128 devices in a mesh: dp: 8 (over z_lo, x), fsdp: 16 (over y, z_hi, core).
Axes of the slice: x: 4, y: 4, z: 4 (z_hi: 2, z_lo: 2; z = z_hi * 2 + z_lo), core: 2. Of those that a mesh axis runs over, the one named last changes fastest.
Arguments:
- queries: bfloat16 [65536, 2048], P(('dp', 'fsdp')), may hold values from -6 to 6
- keys: bfloat16 [65536, 2048], P(('dp', 'fsdp')), may hold values from -6 to 6
- values: bfloat16 [65536, 2048], P(('dp', 'fsdp')), may hold values from -6 to 6
- attn_out: bfloat16 [65536, 2048], P(('dp', 'fsdp')), may hold values from -24 to 24
- out_grad: bfloat16 [65536, 2048], P(('dp', 'fsdp')), may hold values from -6 to 6
- log_norm: float32 [65536, 16], P(('dp', 'fsdp')), may hold values from 4 to 7
- segment_ids: int32 [128, 4], P(('dp', 'fsdp')), may hold values from 0 to 3, as said below
- kept_tokens: int32 [128, 4], P(('dp', 'fsdp')), may hold values from 0 to 512, as said below
- out_weight: bfloat16 [2048, 2048], P('fsdp'), may hold values from -0.125 to 0.125
Outputs:
- query_grad: bfloat16 [65536, 2048], P(('dp', 'fsdp'))
- key_grad: bfloat16 [65536, 2048], P(('dp', 'fsdp'))
- value_grad: bfloat16 [65536, 2048], P(('dp', 'fsdp'))
- weight_grad: float32 [2048, 2048], P('fsdp')
The draws below stay inside these ranges and needn't reach their ends.
Inputs may be any that keep to these rules, and one draw needn't show every extreme that they name: `segment_ids`: row p numbers the images of pack p block by block: 0 for block 0, rising by one at each block that starts a new image. Some pack is one image, some pack has one image a block. `kept_tokens`: entry (p, i) counts the kept tokens of image i of pack p, which fill the start of that image's blocks: an image of b blocks keeps 128 (b - 1) + 1 to 128 b tokens; numbers with no image hold 0.
All inputs are finite; a program needn't handle non-finite values.
Results may differ from the reference program's by a relative error of at most 0.012.
The reference program's roundings to bfloat16 on the way count: a program that leaves them out, or rounds other values in their place, can miss the bound.
Values may be sent and summed in bfloat16 or wider, within the bound.
A program may use at most 192 MiB of HBM per device.

```python
import jax
import jax.numpy as jnp
from jax import lax

HEADS = 16
HEAD_DIM = 128
DW = 2048
BLOCK = 128
TOK_DEV = 512
HW = 2048
BLOCKS = 4
PACKS = 128
TOKENS = 65536


def image_starts(key):
    starts = jax.random.randint(key, (PACKS, BLOCKS), 0, 2).astype(jnp.int32)
    starts = starts.at[:, 0].set(1)
    starts = starts.at[0, 1:].set(0)
    starts = starts.at[1, :].set(1)
    return starts


def draw_segment_ids(key, part):
    starts = image_starts(key)
    return (jnp.cumsum(starts, axis=1) - 1).astype(jnp.int32)


def draw_kept_tokens(key, part):
    starts = image_starts(key)
    key = jax.random.fold_in(key, 23)
    seg_ids = jnp.cumsum(starts, axis=1) - 1
    image_ids = jnp.arange(BLOCKS).astype(jnp.int32)
    block_counts = jnp.sum((seg_ids[:, :, None] == image_ids[None, None, :]).astype(jnp.int32), axis=1)
    extra = jax.random.randint(key, (PACKS, BLOCKS), 1, BLOCK + 1).astype(jnp.int32)
    extra = extra.at[0, 0].set(BLOCK)
    kept_counts = jnp.where(block_counts > 0, (block_counts - 1) * BLOCK + extra, 0)
    return kept_counts.astype(jnp.int32)


def raised(entries, own_key, source, target, shards_of, factor):
    def block_of(position):
        return (jnp.arange(entries.shape[position]) // (entries.shape[position] // shards_of)).reshape((-1,) + (1,) * (entries.ndim - 1 - position))

    one_side = jax.random.permutation(own_key, shards_of)[block_of(target)]
    second = (block_of(target) + shards_of // 2) % shards_of
    return jnp.where((block_of(source) == one_side) | (block_of(source) == second), factor * entries, entries)


def block_scale(key, dims, shards, low, largest):
    def one(axis_at, parts):
        heights = jax.random.uniform(jax.random.fold_in(jax.random.fold_in(key, 6), axis_at), (parts,), jnp.float32, low / len(shards), largest / len(shards))
        return jnp.repeat(jnp.exp(heights), dims[axis_at] // parts).reshape((-1,) + (1,) * (len(dims) - axis_at - 1))

    loudness = one(*shards[0])
    for cut in shards[1:]:
        loudness = loudness * one(*cut)
    return loudness


def scatter_about(stream_key, dims, width, reach, shards=(), dtype=jnp.bfloat16):
    array = jax.random.normal(stream_key, dims, jnp.float32) * width
    if len(shards) > 0:
        array = block_scale(stream_key, dims, shards, -0.22, 0.18) * array
    return jnp.clip(array, min=-reach, max=reach).astype(dtype)


def heavy_noise(own_key, extent, deviation, limit, cuts, heavy, dtype=jnp.bfloat16):
    array = deviation * jax.random.normal(own_key, extent, jnp.float32)
    if cuts:
        array = array * block_scale(own_key, extent, cuts, -0.22, 0.18)
    return jnp.clip(raised(array, jax.random.fold_in(own_key, 3), *heavy), -limit, limit).astype(dtype)


def setup_inputs(seed: int = 0) -> dict:
    streams_of = jax.random.split(jax.random.key(seed), 10)
    return {
        "queries": scatter_about(streams_of[0], (TOKENS, HW), 1.0, 6.0, ((0, 128),)),
        "keys": scatter_about(streams_of[1], (TOKENS, HW), 1.0, 6.0, ((0, 128),)),
        "values": scatter_about(streams_of[2], (TOKENS, HW), 1.0, 6.0, ((0, 128),)),
        "attn_out": heavy_noise(streams_of[3], (TOKENS, HW), 1.0, 24.0, ((0, 128),), (0, 1, 128, 5.5)),
        "out_grad": scatter_about(streams_of[4], (TOKENS, DW), 1.0, 6.0, ((0, 128),)),
        "log_norm": jnp.clip(4.0 + 3.0 * jax.random.uniform(streams_of[5], (TOKENS, HEADS), jnp.float32) ** block_scale(streams_of[5], (TOKENS, HEADS), ((0, 128),), -0.2, 0.2), 4.0, 7.0),
        "segment_ids": draw_segment_ids(jax.random.fold_in(streams_of[9], 71), 0),
        "kept_tokens": draw_kept_tokens(jax.random.fold_in(streams_of[9], 71), 0),
        "out_weight": scatter_about(streams_of[8], (HW, DW), DW ** -0.5, 0.125, ((0, 16),)),
    }


def one_pack(packed):
    query_rows, key_rows, value_rows, grad_rows, token_image, valid_rows, norm_rows, delta_rows = packed
    score_scale = HEAD_DIM ** -0.5
    query_heads = query_rows.astype(jnp.float32).reshape(TOK_DEV, HEADS, HEAD_DIM)
    key_heads = key_rows.astype(jnp.float32).reshape(TOK_DEV, HEADS, HEAD_DIM)
    value_heads = value_rows.astype(jnp.float32).reshape(TOK_DEV, HEADS, HEAD_DIM)
    grad_heads = grad_rows.astype(jnp.float32).reshape(TOK_DEV, HEADS, HEAD_DIM)
    allowed = (token_image[:, None] == token_image[None, :]) & valid_rows[None, :]
    scores = jnp.einsum("qhd,khd->hqk", query_heads, key_heads) * score_scale
    probs = jnp.where(allowed[None, :, :], jnp.exp(scores - norm_rows.T[:, :, None]), jnp.float32(0.0))
    rounded = lax.optimization_barrier(probs.astype(jnp.bfloat16)).astype(jnp.float32)
    value_grad = jnp.einsum("hqk,qhd->khd", rounded, grad_heads)
    prob_grad = jnp.einsum("qhd,khd->hqk", grad_heads, value_heads)
    score_grad = probs * (prob_grad - delta_rows.T[:, :, None])
    score_grad = lax.optimization_barrier(score_grad.astype(jnp.bfloat16)).astype(jnp.float32)
    query_grad = jnp.einsum("hqk,khd->qhd", score_grad, key_heads) * score_scale
    key_grad = jnp.einsum("hqk,qhd->khd", score_grad, query_heads) * score_scale
    return (query_grad.reshape(TOK_DEV, HW).astype(jnp.bfloat16),
            key_grad.reshape(TOK_DEV, HW).astype(jnp.bfloat16),
            value_grad.reshape(TOK_DEV, HW).astype(jnp.bfloat16))


def reference(queries, keys, values, attn_out, out_grad, log_norm, segment_ids, kept_tokens, out_weight):
    block_ids = jnp.arange(BLOCKS).astype(jnp.int32)
    first_block = jnp.sum((segment_ids[:, None, :] < segment_ids[:, :, None]).astype(jnp.int32), axis=2)
    block_kept = jnp.sum((segment_ids[:, :, None] == block_ids[None, None, :]).astype(jnp.int32) * kept_tokens[:, None, :], axis=2)
    positions = (block_ids[None, :] - first_block)[:, :, None] * BLOCK + jnp.arange(BLOCK).astype(jnp.int32)[None, None, :]
    token_valid = (positions < block_kept[:, :, None]).reshape(TOKENS)
    grad_input = jnp.where(token_valid[:, None], out_grad, jnp.zeros_like(out_grad))
    attn_grad = jnp.dot(grad_input, out_weight.T, preferred_element_type=jnp.float32).astype(jnp.bfloat16)
    weight_grad = jnp.dot(attn_out.T, grad_input, preferred_element_type=jnp.float32)
    delta = jnp.sum((attn_grad.astype(jnp.float32) * attn_out.astype(jnp.float32)).reshape(TOKENS, HEADS, HEAD_DIM), axis=2)
    token_image = jnp.repeat(segment_ids, BLOCK, axis=1)
    packed = (queries.reshape(PACKS, TOK_DEV, HW), keys.reshape(PACKS, TOK_DEV, HW),
              values.reshape(PACKS, TOK_DEV, HW), attn_grad.reshape(PACKS, TOK_DEV, HW),
              token_image, token_valid.reshape(PACKS, TOK_DEV),
              log_norm.reshape(PACKS, TOK_DEV, HEADS), delta.reshape(PACKS, TOK_DEV, HEADS))
    query_grad, key_grad, value_grad = lax.map(one_pack, packed)
    return (query_grad.reshape(TOKENS, HW), key_grad.reshape(TOKENS, HW),
            value_grad.reshape(TOKENS, HW), weight_grad)
```

```python
import jax
import jax.numpy as jnp
from jax import lax
from jax.experimental import pallas as pl
from jax.experimental.pallas import tpu as pltpu
from jax.sharding import PartitionSpec as P

T = 512
HW = 2048
HEADS = 16
HR = 128
SH = 8
LOG2E = 1.4426950408889634
F32 = jnp.float32
BF16 = jnp.bfloat16
MESH = pl.DeviceIdType.MESH


def dot_nn(a, b):
    return lax.dot_general(a, b, (((1,), (0,)), ((), ())), preferred_element_type=F32)


def dot_nt(a, b):
    return lax.dot_general(a, b, (((1,), (1,)), ((), ())), preferred_element_type=F32)


def dot_tn(a, b):
    return lax.dot_general(a, b, (((0,), (0,)), ((), ())), preferred_element_type=F32)


def kernel(
    q_hbm, k_hbm, v_hbm, ao_hbm, og_hbm, ln_ref, seg_ref, kept_ref, w_hbm,
    dq_hbm, dk_hbm, dv_hbm, dw_hbm,
    q_v, k_v, v_v, ao, po, g_all, aot, w_all, dwp, d_o, pg, bias, norm_t,
    ra, ta, sa, suma, ya, yra, za,
    rc, tc, sc, sumc, yc, yrc, xc,
    fin, fin_all, dw_v,
    load_sem, out_sem,
    s_core, r_core, r_pg,
    s_a, r_a1, r_ay, r_ax, r_ax2,
    s_c, r_cy, r_cz, r_cz2,
    s_rs, r_ra, r_sa, r_ya, r_za, r_rc, r_sc, r_yc, r_xc, r_fin,
):
    dp = lax.axis_index("dp")
    fs = lax.axis_index("fsdp")
    x = lax.rem(dp, 4)
    zl = lax.div(dp, 4)
    core = lax.rem(fs, 2)
    zh = lax.rem(lax.div(fs, 2), 2)
    y = lax.div(fs, 4)
    z = 2 * zh + zl
    k0 = 2 * y + zh
    zn = 3 - z

    def m4(a):
        return lax.rem(a + 8, 4)

    def dev(x_, y_, z_, c_):
        return (lax.rem(z_, 2) * 4 + x_, (y_ * 2 + lax.div(z_, 2)) * 2 + c_)

    me_partner = dev(x, y, z, 1 - core)

    def at_x(e):
        return dev(m4(x + e), y, z, core)

    def at_y(e):
        return dev(x, m4(y + e), z, core)

    def at_z(e):
        return dev(x, y, m4(z + e), core)

    def cols_a(x_):
        return pl.ds(pl.multiple_of(x_ * 256, 128), 256)

    def cols_c(zl_):
        return pl.ds(pl.multiple_of(1024 + zl_ * 512, 128), 512)

    def head_cols(h):
        return pl.ds(pl.multiple_of(h * HR, HR), HR)

    def rcopy(src, dst, ssem, rsem, to):
        return pltpu.make_async_remote_copy(src, dst, ssem, rsem, device_id=to, device_id_type=MESH)

    def arrived(dst, rsem):
        rcopy(dst, dst, rsem, rsem, me_partner).wait_recv()

    loads = {}

    def load(i, src, dst):
        c = pltpu.make_async_copy(src, dst, load_sem.at[i])
        c.start()
        loads[i] = c

    load(0, w_hbm, w_all.at[k0])
    load(1, og_hbm, g_all.at[pl.ds(0, T)])
    load(2, ao_hbm, ao)
    load(3, q_hbm, q_v)
    load(4, k_hbm, k_v)
    load(5, v_hbm, v_v)

    peers = [me_partner]
    for e in (1, 2, 3):
        peers += [at_x(e), at_y(e), at_z(e)]
    zs = 2 * zh + (1 - zl)
    final_peers = []
    for e in (0, 1, 2, 3):
        if e:
            final_peers.append(dev(m4(x + e), y, z, core))
        final_peers.append(dev(m4(x + e), y, zs, core))
        if e:
            peers.append(dev(m4(x + e), y, zs, core))
    bar = pltpu.get_barrier_semaphore()
    for p in peers:
        pl.semaphore_signal(bar, inc=1, device_id=p, device_id_type=MESH)
    pl.semaphore_wait(bar, len(peers))

    sent = []

    def send(src, dst, ssem, rsem, to):
        c = rcopy(src, dst, ssem, rsem, to)
        c.start()
        sent.append(c)

    loads[0].wait()
    ax, cz = cols_a(x), cols_c(zl)
    na = [0]

    def sem_a():
        na[0] += 1
        return s_a.at[na[0] - 1]

    nc = [0]

    def sem_c():
        nc[0] += 1
        return s_c.at[nc[0] - 1]

    def a_to_y(k, j):
        part = w_all.at[k, :, ax]
        for e in (1, 3, 2):
            send(part, part, sem_a(), r_ay.at[(4 - e) - 1, j], at_y(e))

    def a_to_x(i, k):
        part = w_all.at[k, :, ax]
        send(part, part, sem_a(), r_ax.at[0, i], at_x(1))
        send(part, part, sem_a(), r_ax.at[1, i], at_x(3))

    def a_relay(i, k):
        lcol, rcol = cols_a(m4(x - 1)), cols_a(m4(x + 1))
        arrived(w_all.at[k, :, lcol], r_ax.at[0, i])
        part = w_all.at[k, pl.ds(0, 64), lcol]
        send(part, part, sem_a(), r_ax2.at[0, i], at_x(1))
        arrived(w_all.at[k, :, rcol], r_ax.at[1, i])
        part = w_all.at[k, pl.ds(64, 64), rcol]
        send(part, part, sem_a(), r_ax2.at[1, i], at_x(3))

    def c_to_z(i, k):
        part = w_all.at[k, :, cz]
        send(part, part, sem_c(), r_cz.at[0, i], at_z(1))
        send(part, part, sem_c(), r_cz.at[1, i], at_z(3))

    def z_cols_rows(e, yy):
        zz = m4(z + e)
        return 2 * yy + lax.div(zz, 2), cols_c(lax.rem(zz, 2))

    def c_relay(i, yy):
        k, c = z_cols_rows(-1, yy)
        arrived(w_all.at[k, :, c], r_cz.at[0, i])
        part = w_all.at[k, pl.ds(0, 64), c]
        send(part, part, sem_c(), r_cz2.at[0, i], at_z(1))
        k, c = z_cols_rows(1, yy)
        arrived(w_all.at[k, :, c], r_cz.at[1, i])
        part = w_all.at[k, pl.ds(64, 64), c]
        send(part, part, sem_c(), r_cz2.at[1, i], at_z(3))

    own_a = w_all.at[k0, :, ax]
    own_c = w_all.at[k0, :, cz]
    k1 = 2 * y + 1 - zh
    send(own_a, own_a, sem_a(), r_a1.at[0], dev(x, y, zn, core))
    send(own_c, own_c, sem_c(), r_cz.at[0, 0], dev(x, y, zn, core))
    send(own_c, own_c, sem_c(), r_cz.at[1, 0], at_z(2))
    a_to_y(k0, 0)
    for e in (1, 3, 2):
        send(own_c, own_c, sem_c(), r_cy.at[(4 - e) - 1], at_y(e))

    loads[1].wait()
    segs = [seg_ref[0, b] for b in range(4)]
    kepts = [kept_ref[0, b] for b in range(4)]
    live = []
    for b in range(4):
        first = jnp.int32(0)
        kept = jnp.int32(0)
        for j in range(4):
            first = first + jnp.where(segs[j] < segs[b], 1, 0)
            kept = kept + jnp.where(segs[b] == j, kepts[j], 0)
        live.append(kept - (b - first) * 128)
    for b in range(4):
        rows = pl.ds(b * 128, 128)
        ok = lax.broadcasted_iota(jnp.int32, (128, HW), 0) < live[b]
        g_all[rows, :] = jnp.where(ok, g_all[rows, :].astype(F32), 0.0).astype(BF16)
    own_g = g_all.at[pl.ds(0, T)]
    send(own_g, g_all.at[pl.ds(T, T)], s_core.at[0], r_core.at[0], me_partner)
    loads[2].wait()
    for i in range(SH):
        send(ao.at[:, head_cols(2 * i + 1 - core)], po.at[i], s_core.at[1 + i], r_core.at[1 + i], me_partner)

    for b in range(4):
        ok = lax.broadcasted_iota(jnp.int32, (128, 128), 0) < live[b]
        for t in range(4):
            same = ok & (jnp.full((128, 128), segs[b] - segs[t]) == 0)
            bias[pl.ds(b * 128, 128), pl.ds(t * 128, 128)] = jnp.where(same, 0.0, -1e30).astype(F32)
    lanes = jnp.concatenate([ln_ref[...] * LOG2E, jnp.zeros((T, 112), F32)], axis=1)
    norm_t[...] = jnp.transpose(lanes)

    for i in range(SH):
        aot[pl.ds(i * HR, HR), pl.ds(0, T)] = jnp.transpose(ao[:, head_cols(2 * i + core)])

    arrived(w_all.at[k1, :, ax], r_a1.at[0])
    a_to_x(1, k1)
    a_to_y(k1, 1)
    arrived(w_all.at[2 * m4(y + 1) + zh, :, cz], r_cy.at[0])
    c_to_z(1, 2 * m4(y + 1) + zh)
    arrived(w_all.at[2 * m4(y + 3) + zh, :, cz], r_cy.at[2])
    c_to_z(2, 2 * m4(y + 3) + zh)

    order_a = [k0, k1]
    for e in (1, 3, 2):
        for j in (0, 1):
            order_a.append(2 * m4(y + e) + (zh if j == 0 else 1 - zh))
    y_of = [y, m4(y + 1), m4(y + 3), m4(y + 2)]

    def a_step(i):
        e = (1, 3, 2)[(i - 2) // 2]
        j = i % 2
        arrived(w_all.at[order_a[i], :, ax], r_ay.at[e - 1, j])
        a_to_x(i, order_a[i])

    a_step(2)
    a_step(4)

    for i in range(SH):
        arrived(po.at[i], r_core.at[1 + i])
        aot[pl.ds(i * HR, HR), pl.ds(T, T)] = jnp.transpose(po[i])
    arrived(g_all.at[pl.ds(T, T)], r_core.at[0])

    def dw_tiles(lo, hi):
        def body(n, carry):
            cols = pl.ds(pl.multiple_of(n * 256, 256), 256)
            part = dot_nn(aot[...], g_all[:, cols])
            dwp[:, :, cols] = part.reshape(SH, HR, 256).astype(BF16)
            return carry

        lax.fori_loop(lo, hi, body, 0)

    dw_tiles(0, 3)
    arrived(w_all.at[2 * m4(y + 2) + zh, :, cz], r_cy.at[1])
    c_to_z(3, 2 * m4(y + 2) + zh)
    a_step(6)
    a_step(3)
    a_step(5)
    a_step(7)
    a_relay(1, order_a[1])
    c_relay(1, y_of[1])
    dw_tiles(3, 6)
    c_relay(2, y_of[2])
    a_relay(2, order_a[2])
    a_relay(4, order_a[4])
    a_relay(6, order_a[6])
    dw_tiles(6, 8)
    for i in (3, 5, 7):
        a_relay(i, order_a[i])
    c_relay(3, y_of[3])

    nr = [0]

    def sem_rs():
        nr[0] += 1
        return s_rs.at[nr[0] - 1]

    dwz = dwp
    half = (pl.ds(0, 4), pl.ds(4, 4))
    xr, xl, x2 = m4(x + 1), m4(x + 3), m4(x + 2)
    send(dwz.at[half[0], :, cols_a(x2)], ra.at[0], sem_rs(), r_ra.at[0], at_x(1))
    send(dwz.at[half[1], :, cols_a(x2)], ra.at[1], sem_rs(), r_ra.at[1], at_x(3))

    def c_rows(e, hf):
        zz = m4(z + e)
        return lax.div(zz, 2), cols_c(lax.rem(zz, 2))

    def send_c(e, ys, dst, base, rsem, r0, to):
        zhh, c = c_rows(e, None)
        for n, yy in enumerate(ys):
            send(dwz.at[2 * yy + zhh, :, c], dst.at[base + n], sem_rs(), rsem.at[r0 + n], to)

    send_c(2, (0, 1), rc.at[0], 0, r_rc, 0, at_z(1))
    send_c(2, (2, 3), rc.at[1], 0, r_rc, 2, at_z(3))
    send(dwz.at[half[1], :, cols_a(xr)], sa.at[0, half[1]], sem_rs(), r_sa.at[0, 1], at_x(1))
    send(dwz.at[half[0], :, cols_a(xl)], sa.at[1, half[0]], sem_rs(), r_sa.at[1, 0], at_x(3))
    send_c(1, (2, 3), sc.at[0], 2, r_sc, 2, at_z(1))
    send_c(3, (0, 1), sc.at[1], 0, r_sc, 4, at_z(3))

    for i in range(1, 8):
        k = order_a[i]
        arrived(w_all.at[k, pl.ds(0, 64), cols_a(m4(x + 2))], r_ax2.at[0, i])
        arrived(w_all.at[k, pl.ds(64, 64), cols_a(m4(x + 2))], r_ax2.at[1, i])
    arrived(w_all.at[k1, :, cols_c(1 - zl)], r_cz.at[0, 0])
    arrived(w_all.at[k1, :, cz], r_cz.at[1, 0])
    for i in range(1, 4):
        k, c = z_cols_rows(2, y_of[i])
        arrived(w_all.at[k, pl.ds(0, 64), c], r_cz2.at[0, i])
        arrived(w_all.at[k, pl.ds(64, 64), c], r_cz2.at[1, i])

    for i in range(4):
        wt = w_all[pl.ds(2 * i, 2)].reshape(2 * HR, HW)
        for part in (1, 0):
            got = dot_nt(g_all[pl.ds(part * T, T), :], wt).astype(BF16)
            for j in range(2):
                piece = got[:, j * HR : (j + 1) * HR]
                if part == 0:
                    d_o[2 * (2 * i + j) + core] = piece
                else:
                    pg[2 * i + j] = piece
                    send(pg.at[2 * i + j], d_o.at[2 * (2 * i + j) + core], s_core.at[9 + 2 * i + j], r_pg.at[2 * i + j], me_partner)

    scale = HR ** -0.5
    loads[3].wait()
    loads[4].wait()
    loads[5].wait()

    def attention(parity, lo, hi):
        def body(i, carry):
            h = 2 * i + parity
            hc = head_cols(h)
            qh, kh, vh = q_v[:, hc], k_v[:, hc], v_v[:, hc]
            gh = d_o[h]
            both = gh.astype(F32) * ao[:, hc].astype(F32)
            delta = jnp.sum(jnp.transpose(both), axis=0, keepdims=True)
            norm = norm_t[pl.ds(h, 1), :]
            s = dot_nt(kh, qh) * (scale * LOG2E) - norm + bias[...]
            p = jnp.exp2(s)
            dv = dot_nn(p.astype(BF16), gh)
            ds = (p * (dot_nt(vh, gh) - delta)).astype(BF16)
            dk = dot_nn(ds, qh) * scale
            dq = dot_tn(ds, kh) * scale
            q_v[:, hc] = dq.astype(BF16)
            k_v[:, hc] = dk.astype(BF16)
            v_v[:, hc] = dv.astype(BF16)
            return carry

        lax.fori_loop(lo, hi, body, 0)

    attention(core, 0, 2)

    def relay_a(d):
        arrived(ra.at[d], r_ra.at[d])
        to = xr if d == 0 else xl
        ta[d] = (dwp[half[d], :, cols_a(to)].astype(F32) + ra[d].astype(F32)).astype(BF16)
        send(ta.at[d], sa.at[d, half[d]], sem_rs(), r_sa.at[d, d], at_x(1 if d == 0 else 3))

    def relay_c(d):
        zhh, c = c_rows(1 if d == 0 else 3, None)
        for n in range(2):
            yy = 2 * d + n
            arrived(rc.at[d, n], r_rc.at[2 * d + n])
            tc[d, n] = (dwp[2 * yy + zhh, :, c].astype(F32) + rc[d, n].astype(F32)).astype(BF16)
            send(tc.at[d, n], sc.at[d, yy], sem_rs(), r_sc.at[4 * d + yy], at_z(1 if d == 0 else 3))

    for d in (0, 1):
        relay_a(d)
        relay_c(d)

    attention(core, 2, 7)

    for d in (0, 1):
        arrived(sa.at[d, half[0]], r_sa.at[d, 0])
        arrived(sa.at[d, half[1]], r_sa.at[d, 1])
    for yy in range(4):
        rows = pl.ds(2 * yy, 2)
        suma[rows] = (
            dwp[rows, :, ax].astype(F32) + sa[0, rows].astype(F32) + sa[1, rows].astype(F32)
        ).astype(BF16)
    for e in (1, 3, 2):
        rows = pl.ds(2 * m4(y + e), 2)
        send(suma.at[rows], ya.at[(4 - e) - 1], sem_rs(), r_ya.at[(4 - e) - 1], at_y(e))
    for d in (0, 1):
        for yy in range(4):
            arrived(sc.at[d, yy], r_sc.at[4 * d + yy])
    for yy in range(4):
        sumc[yy] = (
            dwp[2 * yy + zh, :, cz].astype(F32) + sc[0, yy].astype(F32) + sc[1, yy].astype(F32)
        ).astype(BF16)
    for e in (1, 3, 2):
        send(sumc.at[m4(y + e)], yc.at[(4 - e) - 1], sem_rs(), r_yc.at[(4 - e) - 1], at_y(e))

    attention(core, 7, 8)
    for i in range(SH):
        arrived(d_o.at[2 * i + 1 - core], r_pg.at[i])
    attention(1 - core, 0, 2)

    for e in (1, 2, 3):
        arrived(ya.at[e - 1], r_ya.at[e - 1])
        arrived(yc.at[e - 1], r_yc.at[e - 1])
    tot = suma[pl.ds(2 * y, 2)].astype(F32)
    totc = sumc[y].astype(F32)
    for e in range(3):
        tot = tot + ya[e].astype(F32)
        totc = totc + yc[e].astype(F32)
    yra[...] = tot.astype(BF16)
    yrc[...] = totc.astype(BF16)

    def quarter(i):
        return pl.ds(pl.multiple_of(i * HR, HR), HR)

    for e in (1, 3, 2):
        zz = m4(z + e)
        send(yra.at[lax.div(zz, 2), :, quarter(lax.rem(zz, 2))], za.at[(4 - e) - 1], sem_rs(), r_za.at[(4 - e) - 1], at_z(e))
        send(yrc.at[:, quarter(m4(x + e))], xc.at[(4 - e) - 1], sem_rs(), r_xc.at[(4 - e) - 1], at_x(e))

    attention(1 - core, 2, 4)

    for e in range(3):
        arrived(za.at[e], r_za.at[e])
        arrived(xc.at[e], r_xc.at[e])
    tot = yra[zh, :, quarter(zl)].astype(F32)
    totc = yrc[:, quarter(x)].astype(F32)
    for e in range(3):
        tot = tot + za[e].astype(F32)
        totc = totc + xc[e].astype(F32)
    fin[0] = tot.astype(BF16)
    fin[1] = totc.astype(BF16)
    slot = 0
    for e in range(4):
        for f in (0, 1):
            if e == 0 and f == 0:
                continue
            to = dev(m4(x + e), y, z if f == 0 else zs, core)
            at = ((4 - e) % 4) * 2 + f
            send(fin, fin_all.at[at], sem_rs(), r_fin.at[at], to)
            slot += 1

    attention(1 - core, 4, 8)

    for i, (src, dst) in enumerate(((q_v, dq_hbm), (k_v, dk_hbm), (v_v, dv_hbm))):
        pltpu.make_async_copy(src, dst, out_sem.at[i]).start()

    for e in range(4):
        for f in (0, 1):
            at = e * 2 + f
            if at:
                arrived(fin_all.at[at], r_fin.at[at])
                block = fin_all[at]
            else:
                block = fin[...]
            xx = m4(x + e)
            zz = zl if f == 0 else 1 - zl
            dw_v[:, pl.ds(pl.multiple_of(256 * xx + 128 * zz, 128), 128)] = block[0].astype(F32)
            dw_v[:, pl.ds(pl.multiple_of(1024 + 512 * zz + 128 * xx, 128), 128)] = block[1].astype(F32)
    pltpu.make_async_copy(dw_v, dw_hbm, out_sem.at[3]).start()

    for c in sent:
        c.wait_send()
    for i, (src, dst) in enumerate(((q_v, dq_hbm), (k_v, dk_hbm), (v_v, dv_hbm), (dw_v, dw_hbm))):
        pltpu.make_async_copy(src, dst, out_sem.at[i]).wait()


def per_device(queries, keys, values, attn_out, out_grad, log_norm, segment_ids, kept_tokens, out_weight):
    hbm = pl.BlockSpec(memory_space=pl.ANY)
    vmem = pl.BlockSpec(memory_space=pltpu.VMEM)
    smem = pl.BlockSpec(memory_space=pltpu.SMEM)
    dma = pltpu.SemaphoreType.DMA
    tok = jax.ShapeDtypeStruct((T, HW), BF16)
    V = pltpu.VMEM
    scratch = [
        V((T, HW), BF16), V((T, HW), BF16), V((T, HW), BF16),
        V((T, HW), BF16), V((SH, T, HR), BF16),
        V((2 * T, HW), BF16), V((SH * HR, 2 * T), BF16),
        V((SH, HR, HW), BF16), V((SH, HR, HW), BF16),
        V((HEADS, T, HR), BF16), V((SH, T, HR), BF16),
        V((T, T), F32), V((HR, T), F32),
        V((2, 4, HR, 256), BF16), V((2, 4, HR, 256), BF16), V((2, SH, HR, 256), BF16),
        V((SH, HR, 256), BF16), V((3, 2, HR, 256), BF16), V((2, HR, 256), BF16), V((3, HR, HR), BF16),
        V((2, 2, HR, 512), BF16), V((2, 2, HR, 512), BF16), V((2, 4, HR, 512), BF16),
        V((4, HR, 512), BF16), V((3, HR, 512), BF16), V((HR, 512), BF16), V((3, HR, HR), BF16),
        V((2, HR, HR), BF16), V((8, 2, HR, HR), BF16), V((HR, HW), F32),
        dma((6,)), dma((4,)),
        dma((17,)), dma((9,)), dma((8,)),
        dma((48,)), dma((1,)), dma((3, 2)), dma((2, 8)), dma((2, 8)),
        dma((20,)), dma((3,)), dma((2, 4)), dma((2, 4)),
        dma((48,)), dma((2,)), dma((2, 2)), dma((3,)), dma((3,)),
        dma((4,)), dma((8,)), dma((3,)), dma((3,)), dma((8,)),
    ]
    return pl.pallas_call(
        kernel,
        out_shape=(tok, tok, tok, jax.ShapeDtypeStruct((HR, HW), F32)),
        in_specs=[hbm] * 5 + [vmem, smem, smem, hbm],
        out_specs=(hbm,) * 4,
        scratch_shapes=scratch,
        compiler_params=pltpu.CompilerParams(
            collective_id=0, has_side_effects=True, vmem_limit_bytes=62 * 2**20
        ),
    )(queries, keys, values, attn_out, out_grad, log_norm, segment_ids, kept_tokens, out_weight)


def solution(mesh):
    token = P(("dp", "fsdp"), None)
    return jax.shard_map(
        per_device,
        mesh=mesh,
        in_specs=(token,) * 8 + (P("fsdp", None),),
        out_specs=(token, token, token, P("fsdp", None)),
        check_vma=False,
    )
```

```python
import jax
import jax.numpy as jnp
from jax import lax
from jax.experimental import pallas as pl
from jax.experimental.pallas import tpu as pltpu
from jax.sharding import PartitionSpec as P

T = 512
HW = 2048
HEADS = 16
HR = 128
SH = 8
LOG2E = 1.4426950408889634
F32 = jnp.float32
BF16 = jnp.bfloat16
MESH = pl.DeviceIdType.MESH


def dot_nn(a, b):
    return lax.dot_general(a, b, (((1,), (0,)), ((), ())), preferred_element_type=F32)


def dot_nt(a, b):
    return lax.dot_general(a, b, (((1,), (1,)), ((), ())), preferred_element_type=F32)


def dot_tn(a, b):
    return lax.dot_general(a, b, (((0,), (0,)), ((), ())), preferred_element_type=F32)


def kernel(
    q_hbm, k_hbm, v_hbm, ao_hbm, og_hbm, ln_hbm, seg_hbm, kept_hbm, w_hbm,
    dq_hbm, dk_hbm, dv_hbm, dw_hbm,
    q_v, k_v, v_v, ao, po, g_all, aot, w_all, dwp, d_o, pg, bias, norm_t, seg_ref, kept_ref,
    ra, ta, sa, suma, ya, yra, za,
    rc, tc, sc, sumc, yc, yrc, xc,
    fin, fin_all, dw_v,
    load_sem, out_sem, dw_sem,
    s_core, r_core, r_pg,
    s_a, r_a1, r_ay, r_ax, r_ax2,
    s_c, r_cy, r_cz, r_cz2,
    s_rs, r_ra, r_sa, r_ya, r_za, r_rc, r_sc, r_yc, r_xc, r_fin,
):
    dp = lax.axis_index("dp")
    fs = lax.axis_index("fsdp")
    x = lax.rem(dp, 4)
    zl = lax.div(dp, 4)
    core = lax.rem(fs, 2)
    zh = lax.rem(lax.div(fs, 2), 2)
    y = lax.div(fs, 4)
    z = 2 * zh + zl
    k0 = 2 * y + zh
    zn = 3 - z

    def m4(a):
        return lax.rem(a + 8, 4)

    def dev(x_, y_, z_, c_):
        return (lax.rem(z_, 2) * 4 + x_, (y_ * 2 + lax.div(z_, 2)) * 2 + c_)

    me_partner = dev(x, y, z, 1 - core)

    def at_x(e):
        return dev(m4(x + e), y, z, core)

    def at_y(e):
        return dev(x, m4(y + e), z, core)

    def at_z(e):
        return dev(x, y, m4(z + e), core)

    def cols_a(x_):
        return pl.ds(pl.multiple_of(x_ * 256, 128), 256)

    def cols_c(zl_):
        return pl.ds(pl.multiple_of(1024 + zl_ * 512, 128), 512)

    def head_cols(h):
        return pl.ds(pl.multiple_of(h * HR, HR), HR)

    def rcopy(src, dst, ssem, rsem, to):
        return pltpu.make_async_remote_copy(src, dst, ssem, rsem, device_id=to, device_id_type=MESH)

    def arrived(dst, rsem):
        rcopy(dst, dst, rsem, rsem, me_partner).wait_recv()

    loads = []

    def load(src, dst):
        c = pltpu.make_async_copy(src, dst, load_sem.at[len(loads)])
        c.start()
        loads.append(c)
        return c

    l_w = load(w_hbm, w_all.at[k0])
    l_seg = load(seg_hbm, seg_ref)
    l_kept = load(kept_hbm, kept_ref)
    l_g = load(og_hbm, g_all.at[pl.ds(0, T)])
    l_ao = load(ao_hbm, ao)
    l_ln = load(ln_hbm, norm_t)
    l_q = load(q_hbm, q_v)
    l_k = load(k_hbm, k_v)
    l_v = load(v_hbm, v_v)

    zs = 2 * zh + (1 - zl)
    peers = [me_partner]
    for e in (1, 2, 3):
        peers += [at_x(e), at_y(e), at_z(e), dev(m4(x + e), y, zs, core)]
    bar = pltpu.get_barrier_semaphore()
    for p in peers:
        pl.semaphore_signal(bar, inc=1, device_id=p, device_id_type=MESH)
    pl.semaphore_wait(bar, len(peers))

    sent = []
    used = {"a": 0, "c": 0, "rs": 0}
    send_sems = {"a": s_a, "c": s_c, "rs": s_rs}

    def send(src, dst, ssem, rsem, to):
        if isinstance(ssem, str):
            used[ssem] += 1
            ssem = send_sems[ssem].at[used[ssem] - 1]
        c = rcopy(src, dst, ssem, rsem, to)
        c.start()
        sent.append(c)

    l_w.wait()
    ax, cz = cols_a(x), cols_c(zl)
    k1 = 2 * y + 1 - zh
    ORDER = (1, 3, 2)

    def row_k(e, j):
        return 2 * m4(y + e) + (zh if j == 0 else 1 - zh)

    def a_to_y(k, j, es):
        part = w_all.at[k, :, ax]
        for e in es:
            send(part, part, "a", r_ay.at[(4 - e) - 1, j], at_y(e))

    def c_to_y(es):
        part = w_all.at[k0, :, cz]
        for e in es:
            send(part, part, "c", r_cy.at[(4 - e) - 1], at_y(e))

    def a_to_x(e, j):
        k = row_k(e, j)
        part = w_all.at[k, :, ax]
        send(part, part, "a", r_ax.at[0, e, j], at_x(1))
        send(part, part, "a", r_ax.at[1, e, j], at_x(3))

    def a_relay(e, j):
        k = row_k(e, j)
        lcol, rcol = cols_a(m4(x - 1)), cols_a(m4(x + 1))
        arrived(w_all.at[k, :, lcol], r_ax.at[0, e, j])
        part = w_all.at[k, pl.ds(0, 64), lcol]
        send(part, part, "a", r_ax2.at[0, e, j], at_x(1))
        arrived(w_all.at[k, :, rcol], r_ax.at[1, e, j])
        part = w_all.at[k, pl.ds(64, 64), rcol]
        send(part, part, "a", r_ax2.at[1, e, j], at_x(3))

    def z_place(ez, e):
        zz = m4(z + ez)
        return 2 * m4(y + e) + lax.div(zz, 2), cols_c(lax.rem(zz, 2))

    def c_to_z(e):
        part = w_all.at[row_k(e, 0), :, cz]
        send(part, part, "c", r_cz.at[0, e], at_z(1))
        send(part, part, "c", r_cz.at[1, e], at_z(3))

    def c_relay(e):
        k, c = z_place(-1, e)
        arrived(w_all.at[k, :, c], r_cz.at[0, e])
        part = w_all.at[k, pl.ds(0, 64), c]
        send(part, part, "c", r_cz2.at[0, e], at_z(1))
        k, c = z_place(1, e)
        arrived(w_all.at[k, :, c], r_cz.at[1, e])
        part = w_all.at[k, pl.ds(64, 64), c]
        send(part, part, "c", r_cz2.at[1, e], at_z(3))

    def a_step(e, j):
        arrived(w_all.at[row_k(e, j), :, ax], r_ay.at[e - 1, j])
        a_to_x(e, j)

    def c_step(e):
        arrived(w_all.at[row_k(e, 0), :, cz], r_cy.at[e - 1])
        c_to_z(e)

    own_a = w_all.at[k0, :, ax]
    own_c = w_all.at[k0, :, cz]
    send(own_a, own_a, "a", r_a1.at[0], dev(x, y, zn, core))
    a_to_y(k0, 0, (1, 3))
    c_to_y((1, 3))
    a_to_y(k0, 0, (2,))
    c_to_y((2,))
    send(own_c, own_c, "c", r_cz.at[0, 0], dev(x, y, zn, core))
    send(own_c, own_c, "c", r_cz.at[1, 0], at_z(2))

    l_seg.wait()
    l_kept.wait()
    segs = [seg_ref[0, b] for b in range(4)]
    kepts = [kept_ref[0, b] for b in range(4)]
    live = []
    for b in range(4):
        first = jnp.int32(0)
        kept = jnp.int32(0)
        for j in range(4):
            first = first + jnp.where(segs[j] < segs[b], 1, 0)
            kept = kept + jnp.where(segs[b] == j, kepts[j], 0)
        live.append(kept - (b - first) * 128)
    l_g.wait()
    for b in range(4):
        rows = pl.ds(b * 128, 128)
        ok = lax.broadcasted_iota(jnp.int32, (128, HW), 0) < live[b]
        g_all[rows, :] = jnp.where(ok, g_all[rows, :].astype(F32), 0.0).astype(BF16)
    own_g = g_all.at[pl.ds(0, T)]
    send(own_g, g_all.at[pl.ds(T, T)], s_core.at[0], r_core.at[0], me_partner)
    l_ao.wait()
    for i in range(SH):
        send(ao.at[:, head_cols(2 * i + 1 - core)], po.at[i], s_core.at[1 + i], r_core.at[1 + i], me_partner)

    arrived(w_all.at[k1, :, ax], r_a1.at[0])
    a_to_y(k1, 1, ORDER)
    a_to_x(0, 1)

    def flip_own(lo, hi):
        for i in range(lo, hi):
            aot[pl.ds(i * HR, HR), pl.ds(0, T)] = jnp.transpose(ao[:, head_cols(2 * i + core)])

    flip_own(0, 2)
    a_step(1, 0)
    a_step(3, 0)
    flip_own(2, 4)
    c_step(1)
    c_step(3)
    flip_own(4, 6)
    a_step(2, 0)
    c_step(2)
    a_relay(0, 1)
    flip_own(6, 8)
    a_relay(1, 0)
    a_relay(3, 0)

    def flip_other(lo, hi):
        for i in range(lo, hi):
            arrived(po.at[i], r_core.at[1 + i])
            aot[pl.ds(i * HR, HR), pl.ds(T, T)] = jnp.transpose(po[i])

    arrived(g_all.at[pl.ds(T, T)], r_core.at[0])
    flip_other(0, 4)
    c_relay(1)
    c_relay(3)
    a_step(1, 1)
    a_step(3, 1)
    flip_other(4, 8)
    a_step(2, 1)

    def dw_group(e):
        rows = pl.ds(pl.multiple_of(2 * m4(y + e) * HR, 2 * HR), 2 * HR)

        def body(n, carry):
            cols = pl.ds(pl.multiple_of(n * 512, 512), 512)
            part = dot_nn(aot[rows, :], g_all[:, cols])
            dwp[pl.ds(2 * m4(y + e), 2), :, cols] = part.reshape(2, HR, 512).astype(BF16)
            return carry

        lax.fori_loop(0, 4, body, 0)

    xr, xl, x2 = m4(x + 1), m4(x + 3), m4(x + 2)
    top, low = pl.ds(0, 64), pl.ds(64, 64)

    def hop_far(e):
        for d in (0, 1):
            to_x, to_z = (at_x(1), at_z(1)) if d == 0 else (at_x(3), at_z(3))
            send(dwp.at[2 * m4(y + e) + d, :, cols_a(x2)], ra.at[d, e], "rs", r_ra.at[d, e], to_x)
            k, c = z_place(2, e)
            send(dwp.at[k, top if d == 0 else low, c], rc.at[d, e], "rs", r_rc.at[d, e], to_z)

    def hop_near(e):
        for d in (0, 1):
            to_x, to_z = (at_x(1), at_z(1)) if d == 0 else (at_x(3), at_z(3))
            f = 1 - d
            send(dwp.at[2 * m4(y + e) + f, :, cols_a(xr if d == 0 else xl)], sa.at[d, e, f], "rs", r_sa.at[d, e, f], to_x)
            k, c = z_place(1 if d == 0 else 3, e)
            part = low if d == 0 else top
            send(dwp.at[k, part, c], sc.at[d, e, part], "rs", r_sc.at[d, e, f], to_z)

    def hop_relay(e):
        for d in (0, 1):
            to_x, to_z = (at_x(1), at_z(1)) if d == 0 else (at_x(3), at_z(3))
            arrived(ra.at[d, e], r_ra.at[d, e])
            near = dwp[2 * m4(y + e) + d, :, cols_a(xr if d == 0 else xl)]
            ta[d, e] = (near.astype(F32) + ra[d, e].astype(F32)).astype(BF16)
            send(ta.at[d, e], sa.at[d, e, d], "rs", r_sa.at[d, e, d], to_x)
            arrived(rc.at[d, e], r_rc.at[d, e])
            k, c = z_place(1 if d == 0 else 3, e)
            part = top if d == 0 else low
            tc[d, e] = (dwp[k, part, c].astype(F32) + rc[d, e].astype(F32)).astype(BF16)
            send(tc.at[d, e], sc.at[d, e, part], "rs", r_sc.at[d, e, d], to_z)

    def hop_sum(e):
        for d in (0, 1):
            for f in (0, 1):
                arrived(sa.at[d, e, f], r_sa.at[d, e, f])
        own = dwp[pl.ds(2 * m4(y + e), 2), :, ax]
        suma[e] = (own.astype(F32) + sa[0, e].astype(F32) + sa[1, e].astype(F32)).astype(BF16)
        if e:
            send(suma.at[e], ya.at[(4 - e) - 1], "rs", r_ya.at[(4 - e) - 1], at_y(e))
        for d in (0, 1):
            for f in (0, 1):
                part = top if f == 0 else low
                arrived(sc.at[d, e, part], r_sc.at[d, e, f])
        own = dwp[2 * m4(y + e) + zh, :, cz]
        sumc[e] = (own.astype(F32) + sc[0, e].astype(F32) + sc[1, e].astype(F32)).astype(BF16)
        if e:
            send(sumc.at[e], yc.at[(4 - e) - 1], "rs", r_yc.at[(4 - e) - 1], at_y(e))

    dw_group(2)
    hop_far(2)
    hop_near(2)
    a_relay(2, 0)
    c_relay(2)
    dw_group(1)
    hop_far(1)
    hop_near(1)
    for e in ORDER:
        a_relay(e, 1)
    dw_group(3)
    hop_far(3)
    hop_near(3)
    hop_relay(2)
    dw_group(0)
    hop_far(0)
    hop_near(0)

    for b in range(4):
        ok = lax.broadcasted_iota(jnp.int32, (128, 128), 0) < live[b]
        for t in range(4):
            same = ok & (jnp.full((128, 128), segs[b] - segs[t]) == 0)
            bias[pl.ds(b * 128, 128), pl.ds(t * 128, 128)] = jnp.where(same, 0.0, -1e30).astype(F32)
    l_ln.wait()
    norm_t[...] = norm_t[...] * LOG2E

    far_a = cols_a(x2)
    for e in (0,) + ORDER:
        for j in (0, 1):
            if e or j:
                arrived(w_all.at[row_k(e, j), pl.ds(0, 64), far_a], r_ax2.at[0, e, j])
                arrived(w_all.at[row_k(e, j), pl.ds(64, 64), far_a], r_ax2.at[1, e, j])
    arrived(w_all.at[k1, :, cols_c(1 - zl)], r_cz.at[0, 0])
    arrived(w_all.at[k1, :, cz], r_cz.at[1, 0])
    for e in ORDER:
        k, c = z_place(2, e)
        arrived(w_all.at[k, pl.ds(0, 64), c], r_cz2.at[0, e])
        arrived(w_all.at[k, pl.ds(64, 64), c], r_cz2.at[1, e])

    for i in range(4):
        wt = w_all[pl.ds(2 * i, 2)].reshape(2 * HR, HW)
        for part in (1, 0):
            got = dot_nt(g_all[pl.ds(part * T, T), :], wt).astype(BF16)
            for j in range(2):
                piece = got[:, j * HR : (j + 1) * HR]
                if part == 0:
                    d_o[2 * (2 * i + j) + core] = piece
                else:
                    pg[2 * i + j] = piece
                    send(pg.at[2 * i + j], d_o.at[2 * (2 * i + j) + core], s_core.at[9 + 2 * i + j], r_pg.at[2 * i + j], me_partner)

    scale = HR ** -0.5
    l_q.wait()
    l_k.wait()
    l_v.wait()
    hop_relay(1)

    def attention(parity, lo, hi):
        def body(i, carry):
            h = 2 * i + parity
            hc = head_cols(h)
            qh, kh, vh = q_v[:, hc], k_v[:, hc], v_v[:, hc]
            gh = d_o[h]
            both = gh.astype(F32) * ao[:, hc].astype(F32)
            delta = jnp.sum(jnp.transpose(both), axis=0, keepdims=True)
            norm = norm_t[pl.ds(h, 1), :]
            s = dot_nt(kh, qh) * (scale * LOG2E) - norm + bias[...]
            p = jnp.exp2(s)
            dv = dot_nn(p.astype(BF16), gh)
            ds = (p * (dot_nt(vh, gh) - delta)).astype(BF16)
            dk = dot_nn(ds, qh) * scale
            dq = dot_tn(ds, kh) * scale
            q_v[:, hc] = dq.astype(BF16)
            k_v[:, hc] = dk.astype(BF16)
            v_v[:, hc] = dv.astype(BF16)
            pltpu.make_async_copy(q_v.at[:, hc], dq_hbm.at[:, hc], out_sem.at[0, h]).start()
            pltpu.make_async_copy(k_v.at[:, hc], dk_hbm.at[:, hc], out_sem.at[1, h]).start()
            pltpu.make_async_copy(v_v.at[:, hc], dv_hbm.at[:, hc], out_sem.at[2, h]).start()
            return carry

        lax.fori_loop(lo, hi, body, 0)

    attention(core, 0, 1)
    hop_relay(3)
    hop_sum(2)
    attention(core, 1, 2)
    hop_relay(0)
    attention(core, 2, 4)
    hop_sum(1)
    attention(core, 4, 6)
    hop_sum(3)
    attention(core, 6, 8)
    hop_sum(0)

    for i in range(SH):
        arrived(d_o.at[2 * i + 1 - core], r_pg.at[i])
    attention(1 - core, 0, 1)

    tot = suma[0].astype(F32)
    totc = sumc[0].astype(F32)
    for e in (2, 1, 3):
        arrived(ya.at[e - 1], r_ya.at[e - 1])
        tot = tot + ya[e - 1].astype(F32)
        arrived(yc.at[e - 1], r_yc.at[e - 1])
        totc = totc + yc[e - 1].astype(F32)
    yra[...] = tot.astype(BF16)
    yrc[...] = totc.astype(BF16)

    def quarter(i):
        return pl.ds(pl.multiple_of(i * HR, HR), HR)

    for e in (1, 3, 2):
        zz = m4(z + e)
        send(yra.at[lax.div(zz, 2), :, quarter(lax.rem(zz, 2))], za.at[(4 - e) - 1], "rs", r_za.at[(4 - e) - 1], at_z(e))
        send(yrc.at[:, quarter(m4(x + e))], xc.at[(4 - e) - 1], "rs", r_xc.at[(4 - e) - 1], at_x(e))

    attention(1 - core, 1, 3)

    for e in range(3):
        arrived(za.at[e], r_za.at[e])
        arrived(xc.at[e], r_xc.at[e])
    tot = yra[zh, :, quarter(zl)].astype(F32)
    totc = yrc[:, quarter(x)].astype(F32)
    for e in range(3):
        tot = tot + za[e].astype(F32)
        totc = totc + xc[e].astype(F32)
    fin[0] = tot.astype(BF16)
    fin[1] = totc.astype(BF16)
    for e in range(4):
        for f in (0, 1):
            if e or f:
                at = ((4 - e) % 4) * 2 + f
                send(fin, fin_all.at[at], "rs", r_fin.at[at], dev(m4(x + e), y, z if f == 0 else zs, core))

    attention(1 - core, 3, 8)

    for e in range(4):
        for f in (0, 1):
            at = e * 2 + f
            if at:
                arrived(fin_all.at[at], r_fin.at[at])
                block = fin_all[at]
            else:
                block = fin[...]
            xx = m4(x + e)
            zz = zl if f == 0 else 1 - zl
            dw_v[:, pl.ds(pl.multiple_of(256 * xx + 128 * zz, 128), 128)] = block[0].astype(F32)
            dw_v[:, pl.ds(pl.multiple_of(1024 + 512 * zz + 128 * xx, 128), 128)] = block[1].astype(F32)
    last = pltpu.make_async_copy(dw_v, dw_hbm, dw_sem.at[0])
    last.start()

    for c in sent:
        c.wait_send()
    for h in range(HEADS):
        hc = pl.ds(h * HR, HR)
        for i, (src, dst) in enumerate(((q_v, dq_hbm), (k_v, dk_hbm), (v_v, dv_hbm))):
            pltpu.make_async_copy(src.at[:, hc], dst.at[:, hc], out_sem.at[i, h]).wait()
    last.wait()


def per_device(queries, keys, values, attn_out, out_grad, log_norm, segment_ids, kept_tokens, out_weight):
    hbm = pl.BlockSpec(memory_space=pl.ANY)
    dma = pltpu.SemaphoreType.DMA
    tok = jax.ShapeDtypeStruct((T, HW), BF16)
    V = pltpu.VMEM
    scratch = [
        V((T, HW), BF16), V((T, HW), BF16), V((T, HW), BF16),
        V((T, HW), BF16), V((SH, T, HR), BF16),
        V((2 * T, HW), BF16), V((SH * HR, 2 * T), BF16),
        V((SH, HR, HW), BF16), V((SH, HR, HW), BF16),
        V((HEADS, T, HR), BF16), V((SH, T, HR), BF16),
        V((T, T), F32), V((HEADS, T), F32),
        pltpu.SMEM((1, 4), jnp.int32), pltpu.SMEM((1, 4), jnp.int32),
        V((2, 4, HR, 256), BF16), V((2, 4, HR, 256), BF16), V((2, 4, 2, HR, 256), BF16),
        V((4, 2, HR, 256), BF16), V((3, 2, HR, 256), BF16), V((2, HR, 256), BF16), V((3, HR, HR), BF16),
        V((2, 4, 64, 512), BF16), V((2, 4, 64, 512), BF16), V((2, 4, HR, 512), BF16),
        V((4, HR, 512), BF16), V((3, HR, 512), BF16), V((HR, 512), BF16), V((3, HR, HR), BF16),
        V((2, HR, HR), BF16), V((8, 2, HR, HR), BF16), V((HR, HW), F32),
        dma((9,)), dma((3, HEADS)), dma((1,)),
        dma((17,)), dma((9,)), dma((8,)),
        dma((48,)), dma((1,)), dma((3, 2)), dma((2, 4, 2)), dma((2, 4, 2)),
        dma((24,)), dma((3,)), dma((2, 4)), dma((2, 4)),
        dma((72,)), dma((2, 4)), dma((2, 4, 2)), dma((3,)), dma((3,)),
        dma((2, 4)), dma((2, 4, 2)), dma((3,)), dma((3,)), dma((8,)),
    ]
    return pl.pallas_call(
        kernel,
        out_shape=(tok, tok, tok, jax.ShapeDtypeStruct((HR, HW), F32)),
        in_specs=[hbm] * 9,
        out_specs=(hbm,) * 4,
        scratch_shapes=scratch,
        compiler_params=pltpu.CompilerParams(
            collective_id=0, has_side_effects=True, vmem_limit_bytes=62 * 2**20
        ),
    )(queries, keys, values, attn_out, out_grad, log_norm.T, segment_ids, kept_tokens, out_weight)


def solution(mesh):
    token = P(("dp", "fsdp"), None)
    return jax.shard_map(
        per_device,
        mesh=mesh,
        in_specs=(token,) * 8 + (P("fsdp", None),),
        out_specs=(token, token, token, P("fsdp", None)),
        check_vma=False,
    )
```

```python
import jax
import jax.numpy as jnp
from jax import lax
from jax.experimental import pallas as pl
from jax.experimental.pallas import tpu as pltpu
from jax.sharding import PartitionSpec as P

T = 512
HW = 2048
HEADS = 16
HR = 128
SH = 8
LOG2E = 1.4426950408889634
F32 = jnp.float32
BF16 = jnp.bfloat16
MESH = pl.DeviceIdType.MESH


def dot_nn(a, b):
    return lax.dot_general(a, b, (((1,), (0,)), ((), ())), preferred_element_type=F32)


def dot_nt(a, b):
    return lax.dot_general(a, b, (((1,), (1,)), ((), ())), preferred_element_type=F32)


def dot_tn(a, b):
    return lax.dot_general(a, b, (((0,), (0,)), ((), ())), preferred_element_type=F32)


def kernel(
    q_hbm, k_hbm, v_hbm, ao_hbm, og_hbm, ln_hbm, seg_hbm, kept_hbm, w_hbm,
    q_v, k_v, v_v, dw_v,
    ao, po, g_all, aot, w_all, dwp, d_o, pg, bias, norm_t, seg_ref, kept_ref,
    ra, ta, sa, suma, ya, yra, za,
    rc, tc, sc, sumc, yc, yrc, xc,
    fin, fin_all,
    load_sem,
    s_core, r_core, r_pg,
    s_a, r_a1, r_ay, r_ax, r_ax2,
    s_c, r_cy, r_cz, r_cz2,
    s_rs, r_ra, r_sa, r_ya, r_za, r_rc, r_sc, r_yc, r_xc, r_fin,
):
    dp = lax.axis_index("dp")
    fs = lax.axis_index("fsdp")
    x = lax.rem(dp, 4)
    zl = lax.div(dp, 4)
    core = lax.rem(fs, 2)
    zh = lax.rem(lax.div(fs, 2), 2)
    y = lax.div(fs, 4)
    z = 2 * zh + zl
    k0 = 2 * y + zh
    zn = 3 - z

    def m4(a):
        return lax.rem(a + 8, 4)

    def dev(x_, y_, z_, c_):
        return (lax.rem(z_, 2) * 4 + x_, (y_ * 2 + lax.div(z_, 2)) * 2 + c_)

    me_partner = dev(x, y, z, 1 - core)

    def at_x(e):
        return dev(m4(x + e), y, z, core)

    def at_y(e):
        return dev(x, m4(y + e), z, core)

    def at_z(e):
        return dev(x, y, m4(z + e), core)

    def cols_a(x_):
        return pl.ds(pl.multiple_of(x_ * 256, 128), 256)

    def cols_c(zl_):
        return pl.ds(pl.multiple_of(1024 + zl_ * 512, 128), 512)

    def head_cols(h):
        return pl.ds(pl.multiple_of(h * HR, HR), HR)

    def rcopy(src, dst, ssem, rsem, to):
        return pltpu.make_async_remote_copy(src, dst, ssem, rsem, device_id=to, device_id_type=MESH)

    def arrived(dst, rsem):
        rcopy(dst, dst, rsem, rsem, me_partner).wait_recv()

    loads = []

    def load(src, dst):
        c = pltpu.make_async_copy(src, dst, load_sem.at[len(loads)])
        c.start()
        loads.append(c)
        return c

    l_w = load(w_hbm, w_all.at[k0])
    l_seg = load(seg_hbm, seg_ref)
    l_kept = load(kept_hbm, kept_ref)
    l_g = load(og_hbm, g_all.at[pl.ds(0, T)])
    l_ao = load(ao_hbm, ao)
    l_ln = load(ln_hbm, norm_t)
    l_q = load(q_hbm, q_v)
    l_k = load(k_hbm, k_v)
    l_v = load(v_hbm, v_v)

    zs = 2 * zh + (1 - zl)
    peers = [me_partner]
    for e in (1, 2, 3):
        peers += [at_x(e), at_y(e), at_z(e), dev(m4(x + e), y, zs, core)]
    bar = pltpu.get_barrier_semaphore()
    for p in peers:
        pl.semaphore_signal(bar, inc=1, device_id=p, device_id_type=MESH)
    pl.semaphore_wait(bar, len(peers))

    sent = []
    used = {"a": 0, "c": 0, "rs": 0}
    send_sems = {"a": s_a, "c": s_c, "rs": s_rs}

    def send(src, dst, ssem, rsem, to):
        if isinstance(ssem, str):
            used[ssem] += 1
            ssem = send_sems[ssem].at[used[ssem] - 1]
        c = rcopy(src, dst, ssem, rsem, to)
        c.start()
        sent.append(c)

    l_w.wait()
    ax, cz = cols_a(x), cols_c(zl)
    k1 = 2 * y + 1 - zh
    ORDER = (1, 3, 2)

    def row_k(e, j):
        return 2 * m4(y + e) + (zh if j == 0 else 1 - zh)

    def a_to_y(k, j, es):
        part = w_all.at[k, :, ax]
        for e in es:
            send(part, part, "a", r_ay.at[(4 - e) - 1, j], at_y(e))

    def c_to_y(es):
        part = w_all.at[k0, :, cz]
        for e in es:
            send(part, part, "c", r_cy.at[(4 - e) - 1], at_y(e))

    def a_piece(e, j, x_):
        if e or j:
            return row_k(e, j), cols_a(x_)
        return k1, pl.ds(pl.multiple_of(1024 + x_ * 256, 128), 256)

    def a_to_x(e, j):
        k, c = a_piece(e, j, x)
        part = w_all.at[k, :, c]
        send(part, part, "a", r_ax.at[0, e, j], at_x(1))
        send(part, part, "a", r_ax.at[1, e, j], at_x(3))

    def a_relay(e, j):
        k, lcol = a_piece(e, j, m4(x - 1))
        arrived(w_all.at[k, :, lcol], r_ax.at[0, e, j])
        part = w_all.at[k, pl.ds(0, 64), lcol]
        send(part, part, "a", r_ax2.at[0, e, j], at_x(1))
        k, rcol = a_piece(e, j, m4(x + 1))
        arrived(w_all.at[k, :, rcol], r_ax.at[1, e, j])
        part = w_all.at[k, pl.ds(64, 64), rcol]
        send(part, part, "a", r_ax2.at[1, e, j], at_x(3))

    def z_place(ez, e):
        zz = m4(z + ez)
        return 2 * m4(y + e) + lax.div(zz, 2), cols_c(lax.rem(zz, 2))

    def c_to_z(e):
        part = w_all.at[row_k(e, 0), :, cz]
        send(part, part, "c", r_cz.at[0, e], at_z(1))
        send(part, part, "c", r_cz.at[1, e], at_z(3))

    def c_relay(e):
        k, c = z_place(-1, e)
        arrived(w_all.at[k, :, c], r_cz.at[0, e])
        part = w_all.at[k, pl.ds(0, 64), c]
        send(part, part, "c", r_cz2.at[0, e], at_z(1))
        k, c = z_place(1, e)
        arrived(w_all.at[k, :, c], r_cz.at[1, e])
        part = w_all.at[k, pl.ds(64, 64), c]
        send(part, part, "c", r_cz2.at[1, e], at_z(3))

    def a_step(e, j):
        arrived(w_all.at[row_k(e, j), :, ax], r_ay.at[e - 1, j])
        a_to_x(e, j)

    def c_step(e):
        arrived(w_all.at[row_k(e, 0), :, cz], r_cy.at[e - 1])
        c_to_z(e)

    own_a = w_all.at[k0, :, ax]
    own_c = w_all.at[k0, :, pl.ds(pl.multiple_of(1024 + x * 256, 128), 256)]
    send(own_a, own_a, "a", r_a1.at[0], dev(x, y, zn, core))
    c_to_y((1, 3))
    send(own_c, own_c, "a", r_a1.at[1], dev(x, y, zn, core))

    l_seg.wait()
    l_kept.wait()
    segs = [seg_ref[0, b] for b in range(4)]
    kepts = [kept_ref[0, b] for b in range(4)]
    live = []
    for b in range(4):
        first = jnp.int32(0)
        kept = jnp.int32(0)
        for j in range(4):
            first = first + jnp.where(segs[j] < segs[b], 1, 0)
            kept = kept + jnp.where(segs[b] == j, kepts[j], 0)
        live.append(kept - (b - first) * 128)
    l_g.wait()
    for b in range(4):
        rows = pl.ds(b * 128, 128)
        ok = lax.broadcasted_iota(jnp.int32, (128, HW), 0) < live[b]
        g_all[rows, :] = jnp.where(ok, g_all[rows, :].astype(F32), 0.0).astype(BF16)
    own_g = g_all.at[pl.ds(0, T)]
    send(own_g, g_all.at[pl.ds(T, T)], s_core.at[0], r_core.at[0], me_partner)
    l_ao.wait()
    for i in range(SH):
        send(ao.at[:, head_cols(2 * i + 1 - core)], po.at[i], s_core.at[1 + i], r_core.at[1 + i], me_partner)

    def flip_own(lo, hi):
        for i in range(lo, hi):
            aot[pl.ds(i * HR, HR), pl.ds(0, T)] = jnp.transpose(ao[:, head_cols(2 * i + core)])

    def flip_other(lo, hi):
        for i in range(lo, hi):
            arrived(po.at[i], r_core.at[1 + i])
            aot[pl.ds(i * HR, HR), pl.ds(T, T)] = jnp.transpose(po[i])

    arrived(w_all.at[k1, :, ax], r_a1.at[0])
    a_to_x(0, 1)
    k, c = a_piece(0, 0, x)
    arrived(w_all.at[k, :, c], r_a1.at[1])
    a_to_x(0, 0)
    c_step(1)
    c_step(3)
    a_to_y(k0, 0, ORDER)
    flip_own(0, 4)
    a_relay(0, 1)
    a_step(1, 0)
    a_step(3, 0)
    a_relay(0, 0)
    a_step(2, 0)
    c_to_y((2,))
    a_to_y(k1, 1, ORDER)
    flip_own(4, 8)
    c_relay(1)
    c_relay(3)
    arrived(g_all.at[pl.ds(T, T)], r_core.at[0])
    flip_other(0, 4)
    a_relay(1, 0)
    a_relay(3, 0)
    flip_other(4, 8)
    c_step(2)
    a_relay(2, 0)
    a_step(1, 1)
    a_step(3, 1)
    a_step(2, 1)

    def dw_group(e):
        rows = pl.ds(pl.multiple_of(2 * m4(y + e) * HR, 2 * HR), 2 * HR)

        def body(n, carry):
            cols = pl.ds(pl.multiple_of(n * 512, 512), 512)
            part = dot_nn(aot[rows, :], g_all[:, cols])
            dwp[pl.ds(2 * m4(y + e), 2), :, cols] = part.reshape(2, HR, 512).astype(BF16)
            return carry

        lax.fori_loop(0, 4, body, 0)

    xr, xl, x2 = m4(x + 1), m4(x + 3), m4(x + 2)
    top, low = pl.ds(0, 64), pl.ds(64, 64)

    def hop_far(e):
        for d in (0, 1):
            to_x, to_z = (at_x(1), at_z(1)) if d == 0 else (at_x(3), at_z(3))
            send(dwp.at[2 * m4(y + e) + d, :, cols_a(x2)], ra.at[d, e], "rs", r_ra.at[d, e], to_x)
            k, c = z_place(2, e)
            send(dwp.at[k, top if d == 0 else low, c], rc.at[d, e], "rs", r_rc.at[d, e], to_z)

    def hop_near(e):
        for d in (0, 1):
            to_x, to_z = (at_x(1), at_z(1)) if d == 0 else (at_x(3), at_z(3))
            f = 1 - d
            send(dwp.at[2 * m4(y + e) + f, :, cols_a(xr if d == 0 else xl)], sa.at[d, e, f], "rs", r_sa.at[d, e, f], to_x)
            k, c = z_place(1 if d == 0 else 3, e)
            part = low if d == 0 else top
            send(dwp.at[k, part, c], sc.at[d, e, part], "rs", r_sc.at[d, e, f], to_z)

    def hop_relay(e):
        for d in (0, 1):
            to_x, to_z = (at_x(1), at_z(1)) if d == 0 else (at_x(3), at_z(3))
            arrived(ra.at[d, e], r_ra.at[d, e])
            near = dwp[2 * m4(y + e) + d, :, cols_a(xr if d == 0 else xl)]
            ta[d, e] = (near.astype(F32) + ra[d, e].astype(F32)).astype(BF16)
            send(ta.at[d, e], sa.at[d, e, d], "rs", r_sa.at[d, e, d], to_x)
            arrived(rc.at[d, e], r_rc.at[d, e])
            k, c = z_place(1 if d == 0 else 3, e)
            part = top if d == 0 else low
            tc[d, e] = (dwp[k, part, c].astype(F32) + rc[d, e].astype(F32)).astype(BF16)
            send(tc.at[d, e], sc.at[d, e, part], "rs", r_sc.at[d, e, d], to_z)

    def hop_sum(e):
        for d in (0, 1):
            for f in (0, 1):
                arrived(sa.at[d, e, f], r_sa.at[d, e, f])
        own = dwp[pl.ds(2 * m4(y + e), 2), :, ax]
        suma[e] = (own.astype(F32) + sa[0, e].astype(F32) + sa[1, e].astype(F32)).astype(BF16)
        if e:
            send(suma.at[e], ya.at[(4 - e) - 1], "rs", r_ya.at[(4 - e) - 1], at_y(e))
        for d in (0, 1):
            for f in (0, 1):
                part = top if f == 0 else low
                arrived(sc.at[d, e, part], r_sc.at[d, e, f])
        own = dwp[2 * m4(y + e) + zh, :, cz]
        sumc[e] = (own.astype(F32) + sc[0, e].astype(F32) + sc[1, e].astype(F32)).astype(BF16)
        if e:
            send(sumc.at[e], yc.at[(4 - e) - 1], "rs", r_yc.at[(4 - e) - 1], at_y(e))

    dw_group(2)
    hop_far(2)
    dw_group(1)
    hop_near(2)
    c_relay(2)
    for e in ORDER:
        a_relay(e, 1)
    hop_far(1)
    dw_group(3)
    dw_group(0)

    for b in range(4):
        ok = lax.broadcasted_iota(jnp.int32, (128, 128), 0) < live[b]
        for t in range(4):
            same = ok & (jnp.full((128, 128), segs[b] - segs[t]) == 0)
            bias[pl.ds(b * 128, 128), pl.ds(t * 128, 128)] = jnp.where(same, 0.0, -1e30).astype(F32)
    l_ln.wait()
    norm_t[...] = norm_t[...] * LOG2E

    hop_relay(2)
    hop_near(1)
    for e in (0,) + ORDER:
        for j in (0, 1):
            k, c = a_piece(e, j, x2)
            arrived(w_all.at[k, pl.ds(0, 64), c], r_ax2.at[0, e, j])
            arrived(w_all.at[k, pl.ds(64, 64), c], r_ax2.at[1, e, j])
    for e in ORDER:
        k, c = z_place(2, e)
        arrived(w_all.at[k, pl.ds(0, 64), c], r_cz2.at[0, e])
        arrived(w_all.at[k, pl.ds(64, 64), c], r_cz2.at[1, e])

    hop_far(3)

    for i in range(4):
        if i == 2:
            hop_relay(1)
            hop_near(3)
            hop_sum(2)
            hop_far(0)
        wt = w_all[pl.ds(2 * i, 2)].reshape(2 * HR, HW)
        for part in (1, 0):
            got = dot_nt(g_all[pl.ds(part * T, T), :], wt).astype(BF16)
            for j in range(2):
                piece = got[:, j * HR : (j + 1) * HR]
                if part == 0:
                    d_o[2 * (2 * i + j) + core] = piece
                else:
                    pg[2 * i + j] = piece
                    send(pg.at[2 * i + j], d_o.at[2 * (2 * i + j) + core], s_core.at[9 + 2 * i + j], r_pg.at[2 * i + j], me_partner)

    scale = HR ** -0.5
    l_q.wait()
    l_k.wait()
    l_v.wait()

    def attention(parity, lo, hi):
        def body(i, carry):
            h = 2 * i + parity
            hc = head_cols(h)
            qh, kh, vh = q_v[:, hc], k_v[:, hc], v_v[:, hc]
            gh = d_o[h]
            both = gh.astype(F32) * ao[:, hc].astype(F32)
            delta = jnp.sum(jnp.transpose(both), axis=0, keepdims=True)
            norm = norm_t[pl.ds(h, 1), :]
            s = dot_nt(kh, qh) * (scale * LOG2E) - norm + bias[...]
            p = jnp.exp2(s)
            dv = dot_nn(p.astype(BF16), gh)
            ds = (p * (dot_nt(vh, gh) - delta)).astype(BF16)
            dk = dot_nn(ds, qh) * scale
            dq = dot_tn(ds, kh) * scale
            q_v[:, hc] = dq.astype(BF16)
            k_v[:, hc] = dk.astype(BF16)
            v_v[:, hc] = dv.astype(BF16)
            return carry

        lax.fori_loop(lo, hi, body, 0)

    attention(core, 0, 2)
    hop_relay(3)
    hop_near(0)
    hop_sum(1)
    attention(core, 2, 6)
    hop_relay(0)
    hop_sum(3)
    attention(core, 6, 8)
    for i in range(SH):
        arrived(d_o.at[2 * i + 1 - core], r_pg.at[i])
    attention(1 - core, 0, 1)
    hop_sum(0)

    tot = suma[0].astype(F32)
    totc = sumc[0].astype(F32)
    for e in (2, 1, 3):
        arrived(ya.at[e - 1], r_ya.at[e - 1])
        tot = tot + ya[e - 1].astype(F32)
        arrived(yc.at[e - 1], r_yc.at[e - 1])
        totc = totc + yc[e - 1].astype(F32)
    yra[...] = tot.astype(BF16)
    yrc[...] = totc.astype(BF16)

    def quarter(i):
        return pl.ds(pl.multiple_of(i * HR, HR), HR)

    for e in (1, 3, 2):
        zz = m4(z + e)
        send(yra.at[lax.div(zz, 2), :, quarter(lax.rem(zz, 2))], za.at[(4 - e) - 1], "rs", r_za.at[(4 - e) - 1], at_z(e))
        send(yrc.at[:, quarter(m4(x + e))], xc.at[(4 - e) - 1], "rs", r_xc.at[(4 - e) - 1], at_x(e))

    attention(1 - core, 1, 4)

    for e in range(3):
        arrived(za.at[e], r_za.at[e])
        arrived(xc.at[e], r_xc.at[e])
    tot = yra[zh, :, quarter(zl)].astype(F32)
    totc = yrc[:, quarter(x)].astype(F32)
    for e in range(3):
        tot = tot + za[e].astype(F32)
        totc = totc + xc[e].astype(F32)
    fin[0] = tot.astype(BF16)
    fin[1] = totc.astype(BF16)
    for e in range(4):
        for f in (0, 1):
            if e or f:
                at = ((4 - e) % 4) * 2 + f
                send(fin, fin_all.at[at], "rs", r_fin.at[at], dev(m4(x + e), y, z if f == 0 else zs, core))

    attention(1 - core, 4, 8)

    for e in range(4):
        for f in (0, 1):
            at = e * 2 + f
            if at:
                arrived(fin_all.at[at], r_fin.at[at])
                block = fin_all[at]
            else:
                block = fin[...]
            xx = m4(x + e)
            zz = zl if f == 0 else 1 - zl
            dw_v[:, pl.ds(pl.multiple_of(256 * xx + 128 * zz, 128), 128)] = block[0].astype(F32)
            dw_v[:, pl.ds(pl.multiple_of(1024 + 512 * zz + 128 * xx, 128), 128)] = block[1].astype(F32)

    for c in sent:
        c.wait_send()


def to_hbm(q, k, v, w, dq, dk, dv, dw, sem):
    copies = [pltpu.make_async_copy(a, b, sem.at[i]) for i, (a, b) in enumerate(((q, dq), (k, dk), (v, dv), (w, dw)))]
    for c in copies:
        c.start()
    for c in copies:
        c.wait()


def per_device(queries, keys, values, attn_out, out_grad, log_norm, segment_ids, kept_tokens, out_weight):
    hbm = pl.BlockSpec(memory_space=pl.ANY)
    dma = pltpu.SemaphoreType.DMA
    V = pltpu.VMEM
    tok = V((T, HW), BF16)
    scratch = [
        V((T, HW), BF16), V((SH, T, HR), BF16),
        V((2 * T, HW), BF16), V((SH * HR, 2 * T), BF16),
        V((SH, HR, HW), BF16), V((SH, HR, HW), BF16),
        V((HEADS, T, HR), BF16), V((SH, T, HR), BF16),
        V((T, T), F32), V((HEADS, T), F32),
        pltpu.SMEM((1, 4), jnp.int32), pltpu.SMEM((1, 4), jnp.int32),
        V((2, 4, HR, 256), BF16), V((2, 4, HR, 256), BF16), V((2, 4, 2, HR, 256), BF16),
        V((4, 2, HR, 256), BF16), V((3, 2, HR, 256), BF16), V((2, HR, 256), BF16), V((3, HR, HR), BF16),
        V((2, 4, 64, 512), BF16), V((2, 4, 64, 512), BF16), V((2, 4, HR, 512), BF16),
        V((4, HR, 512), BF16), V((3, HR, 512), BF16), V((HR, 512), BF16), V((3, HR, HR), BF16),
        V((2, HR, HR), BF16), V((8, 2, HR, HR), BF16),
        dma((9,)),
        dma((17,)), dma((9,)), dma((8,)),
        dma((52,)), dma((2,)), dma((3, 2)), dma((2, 4, 2)), dma((2, 4, 2)),
        dma((24,)), dma((3,)), dma((2, 4)), dma((2, 4)),
        dma((72,)), dma((2, 4)), dma((2, 4, 2)), dma((3,)), dma((3,)),
        dma((2, 4)), dma((2, 4, 2)), dma((3,)), dma((3,)), dma((8,)),
    ]
    grads = pl.pallas_call(
        kernel,
        out_shape=(tok, tok, tok, V((HR, HW), F32)),
        in_specs=[hbm] * 9,
        out_specs=(pl.BlockSpec(memory_space=pltpu.VMEM),) * 4,
        scratch_shapes=scratch,
        compiler_params=pltpu.CompilerParams(
            collective_id=0, has_side_effects=True, vmem_limit_bytes=48 * 2**20
        ),
    )(queries, keys, values, attn_out, out_grad, log_norm.T, segment_ids, kept_tokens, out_weight)
    return pl.pallas_call(
        to_hbm,
        out_shape=tuple(jax.ShapeDtypeStruct(g.shape, g.dtype) for g in grads),
        in_specs=[hbm] * 4,
        out_specs=(hbm,) * 4,
        scratch_shapes=[dma((4,))],
        compiler_params=pltpu.CompilerParams(vmem_limit_bytes=2**20),
    )(*grads)


def solution(mesh):
    token = P(("dp", "fsdp"), None)
    return jax.shard_map(
        per_device,
        mesh=mesh,
        in_specs=(token,) * 8 + (P("fsdp", None),),
        out_specs=(token, token, token, P("fsdp", None)),
        check_vma=False,
    )
```

```python
import jax
import jax.numpy as jnp
from jax import lax
from jax.experimental import pallas as pl
from jax.experimental.pallas import tpu as pltpu
from jax.sharding import PartitionSpec as P

T = 512
HW = 2048
HEADS = 16
HR = 128
SH = 8
LOG2E = 1.4426950408889634
F32 = jnp.float32
BF16 = jnp.bfloat16
MESH = pl.DeviceIdType.MESH


def dot_nn(a, b):
    return lax.dot_general(a, b, (((1,), (0,)), ((), ())), preferred_element_type=F32)


def dot_nt(a, b):
    return lax.dot_general(a, b, (((1,), (1,)), ((), ())), preferred_element_type=F32)


def dot_tn(a, b):
    return lax.dot_general(a, b, (((0,), (0,)), ((), ())), preferred_element_type=F32)


def kernel(
    q_hbm, k_hbm, v_hbm, ao_hbm, og_hbm, ln_hbm, seg_hbm, kept_hbm, w_hbm,
    q_v, k_v, v_v, dw_v,
    ao, po, g_all, aot, w_all, dwp, d_o, pg, bias, norm_t, seg_ref, kept_ref,
    ra, ta, sa, suma, ya, yra, za,
    rc, tc, sc, sumc, yc, yrc, xc,
    fin, fin_all,
    load_sem,
    s_core, r_core, r_pg,
    s_a, r_a1, r_ay, r_ax, r_ax2,
    s_c, r_cy, r_cz, r_cz2,
    s_rs, r_ra, r_sa, r_ya, r_za, r_rc, r_sc, r_yc, r_xc, r_fin,
):
    dp = lax.axis_index("dp")
    fs = lax.axis_index("fsdp")
    x = lax.rem(dp, 4)
    zl = lax.div(dp, 4)
    core = lax.rem(fs, 2)
    zh = lax.rem(lax.div(fs, 2), 2)
    y = lax.div(fs, 4)
    z = 2 * zh + zl
    k0 = 2 * y + zh
    zn = 3 - z

    def m4(a):
        return lax.rem(a + 8, 4)

    def dev(x_, y_, z_, c_):
        return (lax.rem(z_, 2) * 4 + x_, (y_ * 2 + lax.div(z_, 2)) * 2 + c_)

    me_partner = dev(x, y, z, 1 - core)

    def at_x(e):
        return dev(m4(x + e), y, z, core)

    def at_y(e):
        return dev(x, m4(y + e), z, core)

    def at_z(e):
        return dev(x, y, m4(z + e), core)

    def cols_a(x_):
        return pl.ds(pl.multiple_of(x_ * 256, 128), 256)

    def cols_c(zl_):
        return pl.ds(pl.multiple_of(1024 + zl_ * 512, 128), 512)

    def head_cols(h):
        return pl.ds(pl.multiple_of(h * HR, HR), HR)

    def rcopy(src, dst, ssem, rsem, to):
        return pltpu.make_async_remote_copy(src, dst, ssem, rsem, device_id=to, device_id_type=MESH)

    def arrived(dst, rsem):
        rcopy(dst, dst, rsem, rsem, me_partner).wait_recv()

    loads = []

    def load(src, dst):
        c = pltpu.make_async_copy(src, dst, load_sem.at[len(loads)])
        c.start()
        loads.append(c)
        return c

    l_w = load(w_hbm, w_all.at[k0])
    l_seg = load(seg_hbm, seg_ref)
    l_kept = load(kept_hbm, kept_ref)
    l_g = load(og_hbm, g_all.at[pl.ds(0, T)])
    l_ao = load(ao_hbm, ao)
    l_ln = load(ln_hbm, norm_t)
    l_q = load(q_hbm, q_v)
    l_k = load(k_hbm, k_v)
    l_v = load(v_hbm, v_v)

    zs = 2 * zh + (1 - zl)
    peers = [me_partner]
    for e in (1, 2, 3):
        peers += [at_x(e), at_y(e), at_z(e), dev(m4(x + e), y, zs, core)]
    bar = pltpu.get_barrier_semaphore()
    for p in peers:
        pl.semaphore_signal(bar, inc=1, device_id=p, device_id_type=MESH)
    pl.semaphore_wait(bar, len(peers))

    sent = []
    used = {"a": 0, "c": 0, "rs": 0}
    send_sems = {"a": s_a, "c": s_c, "rs": s_rs}

    def send(src, dst, ssem, rsem, to):
        if isinstance(ssem, str):
            used[ssem] += 1
            ssem = send_sems[ssem].at[used[ssem] - 1]
        c = rcopy(src, dst, ssem, rsem, to)
        c.start()
        sent.append(c)

    l_w.wait()
    ax, cz = cols_a(x), cols_c(zl)
    k1 = 2 * y + 1 - zh
    ORDER = (1, 3, 2)

    def row_k(e, j):
        return 2 * m4(y + e) + (zh if j == 0 else 1 - zh)

    def a_to_y(k, j, es):
        part = w_all.at[k, :, ax]
        for e in es:
            send(part, part, "a", r_ay.at[(4 - e) - 1, j], at_y(e))

    def c_to_y(es):
        part = w_all.at[k0, :, cz]
        for e in es:
            send(part, part, "c", r_cy.at[(4 - e) - 1], at_y(e))

    def a_piece(e, j, x_):
        return row_k(e, j), cols_a(x_)

    def a_to_x(e, j):
        k, c = a_piece(e, j, x)
        part = w_all.at[k, :, c]
        send(part, part, "a", r_ax.at[0, e, j], at_x(1))
        send(part, part, "a", r_ax.at[1, e, j], at_x(3))

    def a_relay(e, j):
        k, lcol = a_piece(e, j, m4(x - 1))
        arrived(w_all.at[k, :, lcol], r_ax.at[0, e, j])
        part = w_all.at[k, pl.ds(0, 64), lcol]
        send(part, part, "a", r_ax2.at[0, e, j], at_x(1))
        k, rcol = a_piece(e, j, m4(x + 1))
        arrived(w_all.at[k, :, rcol], r_ax.at[1, e, j])
        part = w_all.at[k, pl.ds(64, 64), rcol]
        send(part, part, "a", r_ax2.at[1, e, j], at_x(3))

    def z_place(ez, e):
        zz = m4(z + ez)
        return 2 * m4(y + e) + lax.div(zz, 2), cols_c(lax.rem(zz, 2))

    def c_to_z(e):
        part = w_all.at[row_k(e, 0), :, cz]
        send(part, part, "c", r_cz.at[0, e], at_z(1))
        send(part, part, "c", r_cz.at[1, e], at_z(3))

    def c_relay(e):
        k, c = z_place(-1, e)
        arrived(w_all.at[k, :, c], r_cz.at[0, e])
        part = w_all.at[k, pl.ds(0, 64), c]
        send(part, part, "c", r_cz2.at[0, e], at_z(1))
        k, c = z_place(1, e)
        arrived(w_all.at[k, :, c], r_cz.at[1, e])
        part = w_all.at[k, pl.ds(64, 64), c]
        send(part, part, "c", r_cz2.at[1, e], at_z(3))

    def a_step(e, j):
        arrived(w_all.at[row_k(e, j), :, ax], r_ay.at[e - 1, j])
        a_to_x(e, j)

    def c_step(e):
        arrived(w_all.at[row_k(e, 0), :, cz], r_cy.at[e - 1])
        c_to_z(e)

    own_a = w_all.at[k0, :, ax]
    send(own_a, own_a, "a", r_a1.at[0], dev(x, y, zn, core))
    c_to_y((1, 3))

    l_seg.wait()
    l_kept.wait()
    segs = [seg_ref[0, b] for b in range(4)]
    kepts = [kept_ref[0, b] for b in range(4)]
    live = []
    for b in range(4):
        first = jnp.int32(0)
        kept = jnp.int32(0)
        for j in range(4):
            first = first + jnp.where(segs[j] < segs[b], 1, 0)
            kept = kept + jnp.where(segs[b] == j, kepts[j], 0)
        live.append(kept - (b - first) * 128)
    l_g.wait()
    for b in range(4):
        rows = pl.ds(b * 128, 128)
        ok = lax.broadcasted_iota(jnp.int32, (128, HW), 0) < live[b]
        g_all[rows, :] = jnp.where(ok, g_all[rows, :].astype(F32), 0.0).astype(BF16)
    own_g = g_all.at[pl.ds(0, T)]
    send(own_g, g_all.at[pl.ds(T, T)], s_core.at[0], r_core.at[0], me_partner)
    l_ao.wait()
    for i in range(SH):
        send(ao.at[:, head_cols(2 * i + 1 - core)], po.at[i], s_core.at[1 + i], r_core.at[1 + i], me_partner)

    part = w_all.at[k0, :, cols_c(1 - zl)]
    send(part, part, "c", r_cz.at[0, 0], dev(x, y, zn, core))

    def flip_own(lo, hi):
        for i in range(lo, hi):
            aot[pl.ds(i * HR, HR), pl.ds(0, T)] = jnp.transpose(ao[:, head_cols(2 * i + core)])

    def flip_other(lo, hi):
        for i in range(lo, hi):
            arrived(po.at[i], r_core.at[1 + i])
            aot[pl.ds(i * HR, HR), pl.ds(T, T)] = jnp.transpose(po[i])

    arrived(w_all.at[k1, :, ax], r_a1.at[0])
    a_to_x(0, 1)
    c_step(1)
    c_step(3)
    a_to_y(k0, 0, ORDER)
    flip_own(0, 4)
    a_relay(0, 1)
    a_step(1, 0)
    a_step(3, 0)
    a_step(2, 0)
    part = w_all.at[k1, :, cz]
    arrived(part, r_cz.at[0, 0])
    send(part, part, "c", r_cz.at[1, 0], dev(x, y, zs, core))
    c_to_y((2,))
    a_to_y(k1, 1, ORDER)
    flip_own(4, 8)
    c_relay(1)
    c_relay(3)
    arrived(g_all.at[pl.ds(T, T)], r_core.at[0])
    flip_other(0, 4)
    a_relay(1, 0)
    a_relay(3, 0)
    flip_other(4, 8)
    c_step(2)
    a_relay(2, 0)
    a_step(1, 1)
    a_step(3, 1)
    a_step(2, 1)

    def dw_group(e):
        rows = pl.ds(pl.multiple_of(2 * m4(y + e) * HR, 2 * HR), 2 * HR)

        def body(n, carry):
            cols = pl.ds(pl.multiple_of(n * 512, 512), 512)
            part = dot_nn(aot[rows, :], g_all[:, cols])
            dwp[pl.ds(2 * m4(y + e), 2), :, cols] = part.reshape(2, HR, 512).astype(BF16)
            return carry

        lax.fori_loop(0, 4, body, 0)

    xr, xl, x2 = m4(x + 1), m4(x + 3), m4(x + 2)
    top, low = pl.ds(0, 64), pl.ds(64, 64)

    def hop_far(e):
        for d in (0, 1):
            to_x, to_z = (at_x(1), at_z(1)) if d == 0 else (at_x(3), at_z(3))
            send(dwp.at[2 * m4(y + e) + d, :, cols_a(x2)], ra.at[d, e], "rs", r_ra.at[d, e], to_x)
            k, c = z_place(2, e)
            send(dwp.at[k, top if d == 0 else low, c], rc.at[d, e], "rs", r_rc.at[d, e], to_z)

    def hop_near(e):
        for d in (0, 1):
            to_x, to_z = (at_x(1), at_z(1)) if d == 0 else (at_x(3), at_z(3))
            f = 1 - d
            send(dwp.at[2 * m4(y + e) + f, :, cols_a(xr if d == 0 else xl)], sa.at[d, e, f], "rs", r_sa.at[d, e, f], to_x)
            k, c = z_place(1 if d == 0 else 3, e)
            part = low if d == 0 else top
            send(dwp.at[k, part, c], sc.at[d, e, part], "rs", r_sc.at[d, e, f], to_z)

    def hop_relay(e):
        for d in (0, 1):
            to_x, to_z = (at_x(1), at_z(1)) if d == 0 else (at_x(3), at_z(3))
            arrived(ra.at[d, e], r_ra.at[d, e])
            near = dwp[2 * m4(y + e) + d, :, cols_a(xr if d == 0 else xl)]
            ta[d, e] = (near.astype(F32) + ra[d, e].astype(F32)).astype(BF16)
            send(ta.at[d, e], sa.at[d, e, d], "rs", r_sa.at[d, e, d], to_x)
            arrived(rc.at[d, e], r_rc.at[d, e])
            k, c = z_place(1 if d == 0 else 3, e)
            part = top if d == 0 else low
            tc[d, e] = (dwp[k, part, c].astype(F32) + rc[d, e].astype(F32)).astype(BF16)
            send(tc.at[d, e], sc.at[d, e, part], "rs", r_sc.at[d, e, d], to_z)

    def hop_sum_a(e):
        for d in (0, 1):
            for f in (0, 1):
                arrived(sa.at[d, e, f], r_sa.at[d, e, f])
        own = dwp[pl.ds(2 * m4(y + e), 2), :, ax]
        suma[e] = (own.astype(F32) + sa[0, e].astype(F32) + sa[1, e].astype(F32)).astype(BF16)
        if e:
            send(suma.at[e], ya.at[(4 - e) - 1], "rs", r_ya.at[(4 - e) - 1], at_y(e))

    def hop_sum_c(e):
        for d in (0, 1):
            for f in (0, 1):
                part = top if f == 0 else low
                arrived(sc.at[d, e, part], r_sc.at[d, e, f])
        own = dwp[2 * m4(y + e) + zh, :, cz]
        sumc[e] = (own.astype(F32) + sc[0, e].astype(F32) + sc[1, e].astype(F32)).astype(BF16)
        if e:
            send(sumc.at[e], yc.at[(4 - e) - 1], "rs", r_yc.at[(4 - e) - 1], at_y(e))

    def hop_sum(e):
        hop_sum_a(e)
        hop_sum_c(e)

    dw_group(2)
    hop_far(2)
    dw_group(1)
    hop_near(2)
    c_relay(2)
    for e in ORDER:
        a_relay(e, 1)
    hop_far(1)
    dw_group(3)
    dw_group(0)

    for b in range(4):
        ok = lax.broadcasted_iota(jnp.int32, (128, 128), 0) < live[b]
        for t in range(4):
            same = ok & (jnp.full((128, 128), segs[b] - segs[t]) == 0)
            bias[pl.ds(b * 128, 128), pl.ds(t * 128, 128)] = jnp.where(same, 0.0, -1e30).astype(F32)
    l_ln.wait()
    norm_t[...] = norm_t[...] * LOG2E

    hop_relay(2)
    hop_near(1)
    for e in (0,) + ORDER:
        for j in (0, 1):
            if e or j:
                k, c = a_piece(e, j, x2)
                arrived(w_all.at[k, pl.ds(0, 64), c], r_ax2.at[0, e, j])
                arrived(w_all.at[k, pl.ds(64, 64), c], r_ax2.at[1, e, j])
    arrived(w_all.at[k1, :, cols_c(1 - zl)], r_cz.at[1, 0])
    for e in ORDER:
        k, c = z_place(2, e)
        arrived(w_all.at[k, pl.ds(0, 64), c], r_cz2.at[0, e])
        arrived(w_all.at[k, pl.ds(64, 64), c], r_cz2.at[1, e])

    hop_far(3)

    for i in range(4):
        if i == 2:
            hop_relay(1)
            hop_near(3)
            hop_sum(2)
            hop_far(0)
        wt = w_all[pl.ds(2 * i, 2)].reshape(2 * HR, HW)
        for part in (1, 0):
            got = dot_nt(g_all[pl.ds(part * T, T), :], wt).astype(BF16)
            for j in range(2):
                piece = got[:, j * HR : (j + 1) * HR]
                if part == 0:
                    d_o[2 * (2 * i + j) + core] = piece
                else:
                    pg[2 * i + j] = piece
                    send(pg.at[2 * i + j], d_o.at[2 * (2 * i + j) + core], s_core.at[9 + 2 * i + j], r_pg.at[2 * i + j], me_partner)

    scale = HR ** -0.5
    l_q.wait()
    l_k.wait()
    l_v.wait()

    def attention(parity, lo, hi):
        def body(i, carry):
            h = 2 * i + parity
            hc = head_cols(h)
            qh, kh, vh = q_v[:, hc], k_v[:, hc], v_v[:, hc]
            gh = d_o[h]
            both = gh.astype(F32) * ao[:, hc].astype(F32)
            delta = jnp.sum(jnp.transpose(both), axis=0, keepdims=True)
            norm = norm_t[pl.ds(h, 1), :]
            s = dot_nt(kh, qh) * (scale * LOG2E) - norm + bias[...]
            p = jnp.exp2(s)
            dv = dot_nn(p.astype(BF16), gh)
            ds = (p * (dot_nt(vh, gh) - delta)).astype(BF16)
            dk = dot_nn(ds, qh) * scale
            dq = dot_tn(ds, kh) * scale
            q_v[:, hc] = dq.astype(BF16)
            k_v[:, hc] = dk.astype(BF16)
            v_v[:, hc] = dv.astype(BF16)
            return carry

        lax.fori_loop(lo, hi, body, 0)

    attention(core, 0, 2)
    hop_relay(3)
    hop_near(0)
    hop_sum(1)
    attention(core, 2, 6)
    hop_relay(0)
    hop_sum(3)
    attention(core, 6, 8)
    for i in range(SH):
        arrived(d_o.at[2 * i + 1 - core], r_pg.at[i])
    attention(1 - core, 0, 1)
    def quarter(i):
        return pl.ds(pl.multiple_of(i * HR, HR), HR)

    hop_sum_a(0)
    tot = suma[0].astype(F32)
    for e in (2, 1, 3):
        arrived(ya.at[e - 1], r_ya.at[e - 1])
        tot = tot + ya[e - 1].astype(F32)
    yra[...] = tot.astype(BF16)
    for e in (2, 1, 3):
        zz = m4(z + e)
        send(yra.at[lax.div(zz, 2), :, quarter(lax.rem(zz, 2))], za.at[(4 - e) - 1], "rs", r_za.at[(4 - e) - 1], at_z(e))
    hop_sum_c(0)
    tot = sumc[0].astype(F32)
    for e in (2, 1, 3):
        arrived(yc.at[e - 1], r_yc.at[e - 1])
        tot = tot + yc[e - 1].astype(F32)
    yrc[...] = tot.astype(BF16)
    for e in (2, 1, 3):
        send(yrc.at[:, quarter(m4(x + e))], xc.at[(4 - e) - 1], "rs", r_xc.at[(4 - e) - 1], at_x(e))

    attention(1 - core, 1, 3)

    def finished(n, own, parts, sems):
        tot = own.astype(F32)
        for e in range(3):
            arrived(parts.at[e], sems.at[e])
            tot = tot + parts[e].astype(F32)
        fin[n] = tot.astype(BF16)
        for e in (2, 1, 3, 0):
            for f in (1, 0):
                if e or f:
                    at = ((4 - e) % 4) * 2 + f
                    to = dev(m4(x + e), y, z if f == 0 else zs, core)
                    send(fin.at[n], fin_all.at[at, n], "rs", r_fin.at[at, n], to)

    finished(0, yra[zh, :, quarter(zl)], za, r_za)
    finished(1, yrc[:, quarter(x)], xc, r_xc)

    attention(1 - core, 3, 8)

    for e in range(4):
        for f in (0, 1):
            at = e * 2 + f
            if at:
                arrived(fin_all.at[at, 0], r_fin.at[at, 0])
                arrived(fin_all.at[at, 1], r_fin.at[at, 1])
                block = fin_all[at]
            else:
                block = fin[...]
            xx = m4(x + e)
            zz = zl if f == 0 else 1 - zl
            dw_v[:, pl.ds(pl.multiple_of(256 * xx + 128 * zz, 128), 128)] = block[0].astype(F32)
            dw_v[:, pl.ds(pl.multiple_of(1024 + 512 * zz + 128 * xx, 128), 128)] = block[1].astype(F32)

    for c in sent:
        c.wait_send()


def to_hbm(q, k, v, w, dq, dk, dv, dw, sem):
    copies = [pltpu.make_async_copy(a, b, sem.at[i]) for i, (a, b) in enumerate(((q, dq), (k, dk), (v, dv), (w, dw)))]
    for c in copies:
        c.start()
    for c in copies:
        c.wait()


def per_device(queries, keys, values, attn_out, out_grad, log_norm, segment_ids, kept_tokens, out_weight):
    hbm = pl.BlockSpec(memory_space=pl.ANY)
    dma = pltpu.SemaphoreType.DMA
    V = pltpu.VMEM
    tok = V((T, HW), BF16)
    scratch = [
        V((T, HW), BF16), V((SH, T, HR), BF16),
        V((2 * T, HW), BF16), V((SH * HR, 2 * T), BF16),
        V((SH, HR, HW), BF16), V((SH, HR, HW), BF16),
        V((HEADS, T, HR), BF16), V((SH, T, HR), BF16),
        V((T, T), F32), V((HEADS, T), F32),
        pltpu.SMEM((1, 4), jnp.int32), pltpu.SMEM((1, 4), jnp.int32),
        V((2, 4, HR, 256), BF16), V((2, 4, HR, 256), BF16), V((2, 4, 2, HR, 256), BF16),
        V((4, 2, HR, 256), BF16), V((3, 2, HR, 256), BF16), V((2, HR, 256), BF16), V((3, HR, HR), BF16),
        V((2, 4, 64, 512), BF16), V((2, 4, 64, 512), BF16), V((2, 4, HR, 512), BF16),
        V((4, HR, 512), BF16), V((3, HR, 512), BF16), V((HR, 512), BF16), V((3, HR, HR), BF16),
        V((2, HR, HR), BF16), V((8, 2, HR, HR), BF16),
        dma((9,)),
        dma((17,)), dma((9,)), dma((8,)),
        dma((48,)), dma((1,)), dma((3, 2)), dma((2, 4, 2)), dma((2, 4, 2)),
        dma((24,)), dma((3,)), dma((2, 4)), dma((2, 4)),
        dma((80,)), dma((2, 4)), dma((2, 4, 2)), dma((3,)), dma((3,)),
        dma((2, 4)), dma((2, 4, 2)), dma((3,)), dma((3,)), dma((8, 2)),
    ]
    grads = pl.pallas_call(
        kernel,
        out_shape=(tok, tok, tok, V((HR, HW), F32)),
        in_specs=[hbm] * 9,
        out_specs=(pl.BlockSpec(memory_space=pltpu.VMEM),) * 4,
        scratch_shapes=scratch,
        compiler_params=pltpu.CompilerParams(
            collective_id=0, has_side_effects=True, vmem_limit_bytes=48 * 2**20
        ),
    )(queries, keys, values, attn_out, out_grad, log_norm.T, segment_ids, kept_tokens, out_weight)
    return pl.pallas_call(
        to_hbm,
        out_shape=tuple(jax.ShapeDtypeStruct(g.shape, g.dtype) for g in grads),
        in_specs=[hbm] * 4,
        out_specs=(hbm,) * 4,
        scratch_shapes=[dma((4,))],
        compiler_params=pltpu.CompilerParams(vmem_limit_bytes=2**20),
    )(*grads)


def solution(mesh):
    token = P(("dp", "fsdp"), None)
    return jax.shard_map(
        per_device,
        mesh=mesh,
        in_specs=(token,) * 8 + (P("fsdp", None),),
        out_specs=(token, token, token, P("fsdp", None)),
        check_vma=False,
    )
```

```python
import jax
import jax.numpy as jnp
from jax import lax
from jax.experimental import pallas as pl
from jax.experimental.pallas import tpu as pltpu
from jax.sharding import PartitionSpec as P

T = 512
HW = 2048
HEADS = 16
HR = 128
SH = 8
LOG2E = 1.4426950408889634
F32 = jnp.float32
BF16 = jnp.bfloat16
MESH = pl.DeviceIdType.MESH


def dot_nn(a, b):
    return lax.dot_general(a, b, (((1,), (0,)), ((), ())), preferred_element_type=F32)


def dot_nt(a, b):
    return lax.dot_general(a, b, (((1,), (1,)), ((), ())), preferred_element_type=F32)


def dot_tn(a, b):
    return lax.dot_general(a, b, (((0,), (0,)), ((), ())), preferred_element_type=F32)


def kernel(
    q_hbm, k_hbm, v_hbm, ao_hbm, og_hbm, ln_hbm, seg_hbm, kept_hbm, w_hbm,
    q_v, k_v, v_v, dw_v,
    ao, po, g_all, aot, w_all, dwp, d_o, pg, bias, norm_t, seg_ref, kept_ref,
    ra, ta, sa, suma, ya, yra, za,
    rc, tc, sc, sumc, yc, yrc, xc,
    fin, fin_all,
    load_sem,
    s_core, r_core, r_pg,
    s_a, r_a1, r_ay, r_ax, r_ax2,
    s_c, r_cy, r_cz, r_cz2,
    s_rs, r_ra, r_sa, r_ya, r_za, r_rc, r_sc, r_yc, r_xc, r_fin,
):
    dp = lax.axis_index("dp")
    fs = lax.axis_index("fsdp")
    x = lax.rem(dp, 4)
    zl = lax.div(dp, 4)
    core = lax.rem(fs, 2)
    zh = lax.rem(lax.div(fs, 2), 2)
    y = lax.div(fs, 4)
    z = 2 * zh + zl
    k0 = 2 * y + zh
    zn = 3 - z

    def m4(a):
        return lax.rem(a + 8, 4)

    def dev(x_, y_, z_, c_):
        return (lax.rem(z_, 2) * 4 + x_, (y_ * 2 + lax.div(z_, 2)) * 2 + c_)

    me_partner = dev(x, y, z, 1 - core)

    def at_x(e):
        return dev(m4(x + e), y, z, core)

    def at_y(e):
        return dev(x, m4(y + e), z, core)

    def at_z(e):
        return dev(x, y, m4(z + e), core)

    def cols_a(x_):
        return pl.ds(pl.multiple_of(x_ * 256, 128), 256)

    def cols_c(zl_):
        return pl.ds(pl.multiple_of(1024 + zl_ * 512, 128), 512)

    def head_cols(h):
        return pl.ds(pl.multiple_of(h * HR, HR), HR)

    def rcopy(src, dst, ssem, rsem, to):
        return pltpu.make_async_remote_copy(src, dst, ssem, rsem, device_id=to, device_id_type=MESH)

    def arrived(dst, rsem):
        rcopy(dst, dst, rsem, rsem, me_partner).wait_recv()

    loads = []

    def load(src, dst):
        c = pltpu.make_async_copy(src, dst, load_sem.at[len(loads)])
        c.start()
        loads.append(c)
        return c

    l_w = load(w_hbm, w_all.at[k0])
    l_seg = load(seg_hbm, seg_ref)
    l_kept = load(kept_hbm, kept_ref)
    l_g = load(og_hbm, g_all.at[pl.ds(0, T)])
    l_ao = load(ao_hbm, ao)
    l_ln = load(ln_hbm, norm_t)
    l_q = load(q_hbm, q_v)
    l_k = load(k_hbm, k_v)
    l_v = load(v_hbm, v_v)

    zs = 2 * zh + (1 - zl)
    peers = [me_partner]
    for e in (1, 2, 3):
        peers += [at_x(e), at_y(e), at_z(e), dev(m4(x + e), y, zs, core)]
    bar = pltpu.get_barrier_semaphore()
    for p in peers:
        pl.semaphore_signal(bar, inc=1, device_id=p, device_id_type=MESH)
    pl.semaphore_wait(bar, len(peers))

    sent = []
    used = {"a": 0, "c": 0, "rs": 0}
    send_sems = {"a": s_a, "c": s_c, "rs": s_rs}

    def send(src, dst, ssem, rsem, to):
        if isinstance(ssem, str):
            used[ssem] += 1
            ssem = send_sems[ssem].at[used[ssem] - 1]
        c = rcopy(src, dst, ssem, rsem, to)
        c.start()
        sent.append(c)

    l_w.wait()
    ax, cz = cols_a(x), cols_c(zl)
    k1 = 2 * y + 1 - zh
    ORDER = (1, 3, 2)

    def row_k(e, j):
        return 2 * m4(y + e) + (zh if j == 0 else 1 - zh)

    def a_to_y(k, j, es):
        part = w_all.at[k, :, ax]
        for e in es:
            send(part, part, "a", r_ay.at[(4 - e) - 1, j], at_y(e))

    def c_to_y(es):
        part = w_all.at[k0, :, cz]
        for e in es:
            send(part, part, "c", r_cy.at[(4 - e) - 1], at_y(e))

    def a_piece(e, j, x_):
        return row_k(e, j), cols_a(x_)

    def a_to_x(e, j):
        k, c = a_piece(e, j, x)
        part = w_all.at[k, :, c]
        send(part, part, "a", r_ax.at[0, e, j], at_x(1))
        send(part, part, "a", r_ax.at[1, e, j], at_x(3))

    def a_relay(e, j):
        k, lcol = a_piece(e, j, m4(x - 1))
        arrived(w_all.at[k, :, lcol], r_ax.at[0, e, j])
        part = w_all.at[k, pl.ds(0, 64), lcol]
        send(part, part, "a", r_ax2.at[0, e, j], at_x(1))
        k, rcol = a_piece(e, j, m4(x + 1))
        arrived(w_all.at[k, :, rcol], r_ax.at[1, e, j])
        part = w_all.at[k, pl.ds(64, 64), rcol]
        send(part, part, "a", r_ax2.at[1, e, j], at_x(3))

    def z_place(ez, e):
        zz = m4(z + ez)
        return 2 * m4(y + e) + lax.div(zz, 2), cols_c(lax.rem(zz, 2))

    def c_to_z(e):
        part = w_all.at[row_k(e, 0), :, cz]
        send(part, part, "c", r_cz.at[0, e], at_z(1))
        send(part, part, "c", r_cz.at[1, e], at_z(3))

    def c_relay(e):
        k, c = z_place(-1, e)
        arrived(w_all.at[k, :, c], r_cz.at[0, e])
        part = w_all.at[k, pl.ds(0, 64), c]
        send(part, part, "c", r_cz2.at[0, e], at_z(1))
        k, c = z_place(1, e)
        arrived(w_all.at[k, :, c], r_cz.at[1, e])
        part = w_all.at[k, pl.ds(64, 64), c]
        send(part, part, "c", r_cz2.at[1, e], at_z(3))

    def a_step(e, j):
        arrived(w_all.at[row_k(e, j), :, ax], r_ay.at[e - 1, j])
        a_to_x(e, j)

    def c_step(e):
        arrived(w_all.at[row_k(e, 0), :, cz], r_cy.at[e - 1])
        c_to_z(e)

    own_a = w_all.at[k0, :, ax]
    send(own_a, own_a, "a", r_a1.at[0], dev(x, y, zn, core))
    c_to_y((1, 3))

    l_seg.wait()
    l_kept.wait()
    segs = [seg_ref[0, b] for b in range(4)]
    kepts = [kept_ref[0, b] for b in range(4)]
    live = []
    for b in range(4):
        first = jnp.int32(0)
        kept = jnp.int32(0)
        for j in range(4):
            first = first + jnp.where(segs[j] < segs[b], 1, 0)
            kept = kept + jnp.where(segs[b] == j, kepts[j], 0)
        live.append(kept - (b - first) * 128)
    l_g.wait()
    for b in range(4):
        rows = pl.ds(b * 128, 128)
        ok = lax.broadcasted_iota(jnp.int32, (128, HW), 0) < live[b]
        g_all[rows, :] = jnp.where(ok, g_all[rows, :].astype(F32), 0.0).astype(BF16)
    own_g = g_all.at[pl.ds(0, T)]
    send(own_g, g_all.at[pl.ds(T, T)], s_core.at[0], r_core.at[0], me_partner)
    l_ao.wait()
    for i in range(SH):
        send(ao.at[:, head_cols(2 * i + 1 - core)], po.at[i], s_core.at[1 + i], r_core.at[1 + i], me_partner)

    part = w_all.at[k0, :, cols_c(1 - zl)]
    send(part, part, "c", r_cz.at[0, 0], dev(x, y, zn, core))

    def flip_own(lo, hi):
        for i in range(lo, hi):
            aot[pl.ds(i * HR, HR), pl.ds(0, T)] = jnp.transpose(ao[:, head_cols(2 * i + core)])

    def flip_other(lo, hi):
        for i in range(lo, hi):
            arrived(po.at[i], r_core.at[1 + i])
            aot[pl.ds(i * HR, HR), pl.ds(T, T)] = jnp.transpose(po[i])

    arrived(w_all.at[k1, :, ax], r_a1.at[0])
    a_to_x(0, 1)
    c_step(1)
    c_step(3)
    a_to_y(k0, 0, ORDER)
    flip_own(0, 4)
    a_relay(0, 1)
    a_step(1, 0)
    a_step(3, 0)
    a_step(2, 0)
    part = w_all.at[k1, :, cz]
    arrived(part, r_cz.at[0, 0])
    send(part, part, "c", r_cz.at[1, 0], dev(x, y, zs, core))
    c_to_y((2,))
    a_to_y(k1, 1, ORDER)
    flip_own(4, 8)
    c_relay(1)
    c_relay(3)
    arrived(g_all.at[pl.ds(T, T)], r_core.at[0])
    flip_other(0, 4)
    a_relay(1, 0)
    a_relay(3, 0)
    flip_other(4, 8)
    c_step(2)
    a_relay(2, 0)
    a_step(1, 1)
    a_step(3, 1)
    a_step(2, 1)

    def dw_group(e):
        rows = pl.ds(pl.multiple_of(2 * m4(y + e) * HR, 2 * HR), 2 * HR)

        def body(n, carry):
            cols = pl.ds(pl.multiple_of(n * 512, 512), 512)
            part = dot_nn(aot[rows, :], g_all[:, cols])
            dwp[pl.ds(2 * m4(y + e), 2), :, cols] = part.reshape(2, HR, 512).astype(BF16)
            return carry

        lax.fori_loop(0, 4, body, 0)

    xr, xl, x2 = m4(x + 1), m4(x + 3), m4(x + 2)
    top, low = pl.ds(0, 64), pl.ds(64, 64)

    def hop_far(e):
        for d in (0, 1):
            to_x, to_z = (at_x(1), at_z(1)) if d == 0 else (at_x(3), at_z(3))
            send(dwp.at[2 * m4(y + e) + d, :, cols_a(x2)], ra.at[d, e], "rs", r_ra.at[d, e], to_x)
            k, c = z_place(2, e)
            send(dwp.at[k, top if d == 0 else low, c], rc.at[d, e], "rs", r_rc.at[d, e], to_z)

    def hop_near(e):
        for d in (0, 1):
            to_x, to_z = (at_x(1), at_z(1)) if d == 0 else (at_x(3), at_z(3))
            f = 1 - d
            send(dwp.at[2 * m4(y + e) + f, :, cols_a(xr if d == 0 else xl)], sa.at[d, e, f], "rs", r_sa.at[d, e, f], to_x)
            k, c = z_place(1 if d == 0 else 3, e)
            part = low if d == 0 else top
            send(dwp.at[k, part, c], sc.at[d, e, part], "rs", r_sc.at[d, e, f], to_z)

    def hop_relay(e):
        for d in (0, 1):
            to_x, to_z = (at_x(1), at_z(1)) if d == 0 else (at_x(3), at_z(3))
            arrived(ra.at[d, e], r_ra.at[d, e])
            near = dwp[2 * m4(y + e) + d, :, cols_a(xr if d == 0 else xl)]
            ta[d, e] = (near.astype(F32) + ra[d, e].astype(F32)).astype(BF16)
            send(ta.at[d, e], sa.at[d, e, d], "rs", r_sa.at[d, e, d], to_x)
            arrived(rc.at[d, e], r_rc.at[d, e])
            k, c = z_place(1 if d == 0 else 3, e)
            part = top if d == 0 else low
            tc[d, e] = (dwp[k, part, c].astype(F32) + rc[d, e].astype(F32)).astype(BF16)
            send(tc.at[d, e], sc.at[d, e, part], "rs", r_sc.at[d, e, d], to_z)

    def hop_sum_a(e):
        for d in (0, 1):
            for f in (0, 1):
                arrived(sa.at[d, e, f], r_sa.at[d, e, f])
        own = dwp[pl.ds(2 * m4(y + e), 2), :, ax]
        suma[e] = (own.astype(F32) + sa[0, e].astype(F32) + sa[1, e].astype(F32)).astype(BF16)
        if e:
            send(suma.at[e], ya.at[(4 - e) - 1], "rs", r_ya.at[(4 - e) - 1], at_y(e))

    def hop_sum_c(e):
        for d in (0, 1):
            for f in (0, 1):
                part = top if f == 0 else low
                arrived(sc.at[d, e, part], r_sc.at[d, e, f])
        own = dwp[2 * m4(y + e) + zh, :, cz]
        sumc[e] = (own.astype(F32) + sc[0, e].astype(F32) + sc[1, e].astype(F32)).astype(BF16)
        if e:
            send(sumc.at[e], yc.at[(4 - e) - 1], "rs", r_yc.at[(4 - e) - 1], at_y(e))

    def hop_sum(e):
        hop_sum_a(e)
        hop_sum_c(e)

    dw_group(2)
    hop_far(2)
    dw_group(1)
    hop_near(2)
    c_relay(2)
    for e in ORDER:
        a_relay(e, 1)
    hop_far(1)
    dw_group(3)
    dw_group(0)

    for b in range(4):
        ok = lax.broadcasted_iota(jnp.int32, (128, 128), 0) < live[b]
        for t in range(4):
            same = ok & (jnp.full((128, 128), segs[b] - segs[t]) == 0)
            bias[pl.ds(b * 128, 128), pl.ds(t * 128, 128)] = jnp.where(same, 0.0, -1e30).astype(F32)
    l_ln.wait()
    norm_t[...] = norm_t[...] * LOG2E

    hop_relay(2)
    hop_near(1)
    for e in (0,) + ORDER:
        for j in (0, 1):
            if e or j:
                k, c = a_piece(e, j, x2)
                arrived(w_all.at[k, pl.ds(0, 64), c], r_ax2.at[0, e, j])
                arrived(w_all.at[k, pl.ds(64, 64), c], r_ax2.at[1, e, j])
    arrived(w_all.at[k1, :, cols_c(1 - zl)], r_cz.at[1, 0])
    for e in ORDER:
        k, c = z_place(2, e)
        arrived(w_all.at[k, pl.ds(0, 64), c], r_cz2.at[0, e])
        arrived(w_all.at[k, pl.ds(64, 64), c], r_cz2.at[1, e])

    hop_far(3)

    for i in range(4):
        if i == 2:
            hop_relay(1)
            hop_near(3)
            hop_sum(2)
            hop_far(0)
        wt = w_all[pl.ds(2 * i, 2)].reshape(2 * HR, HW)
        for part in (1, 0):
            got = dot_nt(g_all[pl.ds(part * T, T), :], wt).astype(BF16)
            for j in range(2):
                piece = got[:, j * HR : (j + 1) * HR]
                if part == 0:
                    d_o[2 * (2 * i + j) + core] = piece
                else:
                    pg[2 * i + j] = piece
                    send(pg.at[2 * i + j], d_o.at[2 * (2 * i + j) + core], s_core.at[9 + 2 * i + j], r_pg.at[2 * i + j], me_partner)

    scale = HR ** -0.5
    l_q.wait()
    l_k.wait()
    l_v.wait()

    def attention(parity, lo, hi):
        def body(i, carry):
            h = 2 * i + parity
            hc = head_cols(h)
            qh, kh, vh = q_v[:, hc], k_v[:, hc], v_v[:, hc]
            gh = d_o[h]
            both = gh.astype(F32) * ao[:, hc].astype(F32)
            delta = jnp.sum(jnp.transpose(both), axis=0, keepdims=True)
            norm = norm_t[pl.ds(h, 1), :]
            s = dot_nt(kh, qh) * (scale * LOG2E) - norm + bias[...]
            p = jnp.exp2(s)
            dv = dot_nn(p.astype(BF16), gh)
            ds = (p * (dot_nt(vh, gh) - delta)).astype(BF16)
            dk = dot_nn(ds, qh) * scale
            dq = dot_tn(ds, kh) * scale
            q_v[:, hc] = dq.astype(BF16)
            k_v[:, hc] = dk.astype(BF16)
            v_v[:, hc] = dv.astype(BF16)
            return carry

        lax.fori_loop(lo, hi, body, 0)

    attention(core, 0, 1)
    hop_relay(3)
    hop_near(0)
    hop_sum(1)
    attention(core, 1, 4)
    hop_relay(0)
    hop_sum(3)
    attention(core, 4, 8)
    for i in range(SH):
        arrived(d_o.at[2 * i + 1 - core], r_pg.at[i])
    def quarter(i):
        return pl.ds(pl.multiple_of(i * HR, HR), HR)

    hop_sum_a(0)
    tot = suma[0].astype(F32)
    for e in (2, 1, 3):
        arrived(ya.at[e - 1], r_ya.at[e - 1])
        tot = tot + ya[e - 1].astype(F32)
    yra[...] = tot.astype(BF16)
    for e in (2, 1, 3):
        zz = m4(z + e)
        send(yra.at[lax.div(zz, 2), :, quarter(lax.rem(zz, 2))], za.at[(4 - e) - 1], "rs", r_za.at[(4 - e) - 1], at_z(e))
    hop_sum_c(0)
    tot = sumc[0].astype(F32)
    for e in (2, 1, 3):
        arrived(yc.at[e - 1], r_yc.at[e - 1])
        tot = tot + yc[e - 1].astype(F32)
    yrc[...] = tot.astype(BF16)
    for e in (2, 1, 3):
        send(yrc.at[:, quarter(m4(x + e))], xc.at[(4 - e) - 1], "rs", r_xc.at[(4 - e) - 1], at_x(e))

    attention(1 - core, 0, 2)

    def finished(n, own, parts, sems):
        tot = own.astype(F32)
        for e in range(3):
            arrived(parts.at[e], sems.at[e])
            tot = tot + parts[e].astype(F32)
        fin[n] = tot.astype(BF16)
        for e in (2, 1, 3, 0):
            for f in (1, 0):
                if e or f:
                    at = ((4 - e) % 4) * 2 + f
                    to = dev(m4(x + e), y, z if f == 0 else zs, core)
                    send(fin.at[n], fin_all.at[at, n], "rs", r_fin.at[at, n], to)

    finished(0, yra[zh, :, quarter(zl)], za, r_za)
    finished(1, yrc[:, quarter(x)], xc, r_xc)

    attention(1 - core, 2, 8)

    for e in range(4):
        for f in (0, 1):
            at = e * 2 + f
            if at:
                arrived(fin_all.at[at, 0], r_fin.at[at, 0])
                arrived(fin_all.at[at, 1], r_fin.at[at, 1])
                block = fin_all[at]
            else:
                block = fin[...]
            xx = m4(x + e)
            zz = zl if f == 0 else 1 - zl
            dw_v[:, pl.ds(pl.multiple_of(256 * xx + 128 * zz, 128), 128)] = block[0].astype(F32)
            dw_v[:, pl.ds(pl.multiple_of(1024 + 512 * zz + 128 * xx, 128), 128)] = block[1].astype(F32)

    for c in sent:
        c.wait_send()


def to_hbm(q, k, v, w, dq, dk, dv, dw, sem):
    copies = [pltpu.make_async_copy(a, b, sem.at[i]) for i, (a, b) in enumerate(((q, dq), (k, dk), (v, dv), (w, dw)))]
    for c in copies:
        c.start()
    for c in copies:
        c.wait()


def per_device(queries, keys, values, attn_out, out_grad, log_norm, segment_ids, kept_tokens, out_weight):
    hbm = pl.BlockSpec(memory_space=pl.ANY)
    dma = pltpu.SemaphoreType.DMA
    V = pltpu.VMEM
    tok = V((T, HW), BF16)
    scratch = [
        V((T, HW), BF16), V((SH, T, HR), BF16),
        V((2 * T, HW), BF16), V((SH * HR, 2 * T), BF16),
        V((SH, HR, HW), BF16), V((SH, HR, HW), BF16),
        V((HEADS, T, HR), BF16), V((SH, T, HR), BF16),
        V((T, T), F32), V((HEADS, T), F32),
        pltpu.SMEM((1, 4), jnp.int32), pltpu.SMEM((1, 4), jnp.int32),
        V((2, 4, HR, 256), BF16), V((2, 4, HR, 256), BF16), V((2, 4, 2, HR, 256), BF16),
        V((4, 2, HR, 256), BF16), V((3, 2, HR, 256), BF16), V((2, HR, 256), BF16), V((3, HR, HR), BF16),
        V((2, 4, 64, 512), BF16), V((2, 4, 64, 512), BF16), V((2, 4, HR, 512), BF16),
        V((4, HR, 512), BF16), V((3, HR, 512), BF16), V((HR, 512), BF16), V((3, HR, HR), BF16),
        V((2, HR, HR), BF16), V((8, 2, HR, HR), BF16),
        dma((9,)),
        dma((17,)), dma((9,)), dma((8,)),
        dma((48,)), dma((1,)), dma((3, 2)), dma((2, 4, 2)), dma((2, 4, 2)),
        dma((24,)), dma((3,)), dma((2, 4)), dma((2, 4)),
        dma((80,)), dma((2, 4)), dma((2, 4, 2)), dma((3,)), dma((3,)),
        dma((2, 4)), dma((2, 4, 2)), dma((3,)), dma((3,)), dma((8, 2)),
    ]
    grads = pl.pallas_call(
        kernel,
        out_shape=(tok, tok, tok, V((HR, HW), F32)),
        in_specs=[hbm] * 9,
        out_specs=(pl.BlockSpec(memory_space=pltpu.VMEM),) * 4,
        scratch_shapes=scratch,
        compiler_params=pltpu.CompilerParams(
            collective_id=0, has_side_effects=True, vmem_limit_bytes=48 * 2**20
        ),
    )(queries, keys, values, attn_out, out_grad, log_norm.T, segment_ids, kept_tokens, out_weight)
    return pl.pallas_call(
        to_hbm,
        out_shape=tuple(jax.ShapeDtypeStruct(g.shape, g.dtype) for g in grads),
        in_specs=[hbm] * 4,
        out_specs=(hbm,) * 4,
        scratch_shapes=[dma((4,))],
        compiler_params=pltpu.CompilerParams(vmem_limit_bytes=2**20),
    )(*grads)


def solution(mesh):
    token = P(("dp", "fsdp"), None)
    return jax.shard_map(
        per_device,
        mesh=mesh,
        in_specs=(token,) * 8 + (P("fsdp", None),),
        out_specs=(token, token, token, P("fsdp", None)),
        check_vma=False,
    )
```
